32 devices in a mesh: probe: 2 (over y), lon: 4 (over z), lat: 2 (over core), trc: 2 (over x).
Axes of the slice: x: 2, y: 2, z: 4, core: 2. Of those that a mesh axis runs over, the one named last changes fastest.
Arguments:
- probe_signs: int32 [24, 2, 32, 256], P(('probe', 'trc'), None, 'lon', 'lat'), parts along dimension 0, may hold values from 0 to 1
- shift_cells: int32 [2, 256], P(None, 'lat'), may hold values from 1 to 31, as said below
- courant_frac: float32 [2, 256], P(None, 'lat'), may hold values from 0 to 1
- merid_coef: float32 [2, 256], P(None, 'lat'), may hold values from 0 to 0.24
- convect_frac: float32 [32, 256], P('lon', 'lat'), may hold values from 0 to 0.9
- footprint: float32 [32, 256], P('lon', 'lat'), may hold values from 0.3 to 3
- region_id: int32 [32, 256], P('lon', 'lat'), may hold values from 0 to 31
- owner_slots: int32 [32], replicated, may hold values from 0 to 31, each once
- prior_slot: float32 [12, 32], P('trc'), may hold values from 0.0125 to 0.1875
Outputs:
- diag_estimate: float32 [24, 2, 32, 256], P(('probe', 'trc'), None, 'lon', 'lat'), parts along dimension 0
The draws below stay inside these ranges and needn't reach their ends.
There are 2 independent parts, one for each index of `probe`. The reference program is written for one: setup_inputs(seed, part) draws one part's arguments, and reference() takes and returns one part's arrays. A program takes and returns all parts, laid end to end along the dimension named above; an argument that names none is the same for every part. Nothing has to cross between parts.
Inputs may be any that keep to these rules, and one draw needn't show every extreme that they name: `shift_cells`: rows below 32 and from 224 on hold shifts of 8 or more at every level; all other rows hold shifts below 8.
All inputs are finite; a program needn't handle non-finite values.
Results may differ from the reference program's by a relative error of at most 0.00011.
Values sent between devices are 32-bit elements; how exact they have to be, the bound alone decides.
No kernel may reach another device: no remote copies, remote signals or barrier semaphores. Data moves between devices by JAX's collectives and lax.ppermute only.
A program may use at most 64 MiB of HBM per device.

```python
import math
import jax
import jax.numpy as jnp

TR = 12
LEV = 2
LOND = 8
POLAR = 32
NLON = 32
NLAT = 256
REGIONS = 32


def draw_shift_cells(key, part):
    key = jax.random.fold_in(key, 7)
    key_far, key_near = jax.random.split(key)
    rows = jnp.arange(NLAT)[None, :]
    polar = (rows < POLAR) | (rows >= NLAT - POLAR)
    far = jax.random.randint(key_far, (LEV, NLAT), LOND, NLON)
    near = jax.random.randint(key_near, (LEV, NLAT), 1, LOND)
    result = jnp.where(polar, far, near)
    result = result.at[0, 0].set(NLON - 1)
    result = result.at[0, POLAR].set(1)
    return result.astype(jnp.int32)


def with_ends(values, own_key, least, high):
    longest = values.shape.index(max(values.shape))
    spots = []
    for shift in (0, 1):
        where = [jax.random.randint(jax.random.fold_in(own_key, axis), (), 0, length) for axis, length in enumerate(values.shape)]
        where[longest] = (where[longest] + shift) % values.shape[longest]
        spots.append(tuple(where))
    return values.at[spots[0]].set(least).at[spots[1]].set(high)


def levels(rng, extent, cuts, least, high):
    def one(axis_at, parts):
        heights = jax.random.uniform(jax.random.fold_in(jax.random.fold_in(rng, 6), axis_at), (parts,), jnp.float32, least / len(cuts), high / len(cuts))
        return jnp.repeat(jnp.exp(heights), extent[axis_at] // parts).reshape((-1,) + (1,) * (len(extent) - axis_at - 1))

    factor_of = one(*cuts[0])
    for cut in cuts[1:]:
        factor_of = factor_of * one(*cut)
    return factor_of


def setup_inputs(seed: int = 0, part: int = 0) -> dict:
    splits = jax.random.split(jax.random.key(seed), 10)
    part_keys = jax.random.split(jax.random.fold_in(splits[9], part), 10)
    return {
        "probe_signs": with_ends(jax.random.randint(part_keys[0], (TR, LEV, NLON, NLAT), 0, 2), jax.random.fold_in(part_keys[0], 1), 0, 1).astype(jnp.int32),
        "shift_cells": draw_shift_cells(jax.random.fold_in(splits[9], 71), part),
        "courant_frac": jnp.clip(1.0 * jax.random.uniform(splits[2], (LEV, NLAT), jnp.float32) ** levels(splits[2], (LEV, NLAT), ((1, 2),), -0.2, 0.2), 0.0, 1.0),
        "merid_coef": jnp.clip(0.24 * jax.random.uniform(splits[3], (LEV, NLAT), jnp.float32) ** levels(splits[3], (LEV, NLAT), ((1, 2),), -0.2, 0.2), 0.0, 0.24),
        "convect_frac": jnp.clip(0.9 * jax.random.uniform(splits[4], (NLON, NLAT), jnp.float32) ** levels(splits[4], (NLON, NLAT), ((0, 4), (1, 2)), -0.2, 0.2), 0.0, 0.9),
        "footprint": jnp.clip(jnp.exp(math.log(3.0) - 2.3025851 * jax.random.uniform(splits[5], (NLON, NLAT), jnp.float32) ** levels(splits[5], (NLON, NLAT), ((0, 4), (1, 2)), -0.2, 0.2)), 0.3, 3.0),
        "region_id": with_ends(jax.random.randint(splits[6], (NLON, NLAT), 0, REGIONS), jax.random.fold_in(splits[6], 1), 0, REGIONS - 1).astype(jnp.int32),
        "owner_slots": jax.random.permutation(splits[7], REGIONS).astype(jnp.int32),
        "prior_slot": jnp.clip(jnp.exp(math.log(0.1875) - 2.7080502 * jax.random.uniform(splits[8], (TR, REGIONS), jnp.float32) ** levels(splits[8], (TR, REGIONS), ((0, 2),), -0.2, 0.2)), 0.0125, 0.1875),
    }


def zonal_weights(courant_frac):
    frac = courant_frac[None, :, None, :]
    return frac * (frac + 1.0) / 2.0, 1.0 - frac * frac, -frac * (1.0 - frac) / 2.0


def zonal_forward(field, courant_frac, shift_cells):
    w_left, w_centre, w_right = zonal_weights(courant_frac)
    stencil = w_left * jnp.roll(field, 1, axis=2) + w_centre * field + w_right * jnp.roll(field, -1, axis=2)
    cells = jnp.arange(NLON, dtype=jnp.int32)[None, None, :, None]
    places = (cells - shift_cells[None, :, None, :]) % NLON
    places = jnp.broadcast_to(places, stencil.shape).astype(jnp.int32)
    return jnp.take_along_axis(stencil, places, axis=2)


def zonal_adjoint(field, courant_frac, shift_cells):
    w_left, w_centre, w_right = zonal_weights(courant_frac)
    cells = jnp.arange(NLON, dtype=jnp.int32)[None, None, :, None]
    places = (cells + shift_cells[None, :, None, :]) % NLON
    places = jnp.broadcast_to(places, field.shape).astype(jnp.int32)
    moved = jnp.take_along_axis(field, places, axis=2)
    return w_left * jnp.roll(moved, -1, axis=2) + w_centre * moved + w_right * jnp.roll(moved, 1, axis=2)


def meridional(field, faces):
    coef = faces[None, :, None, :]
    zeros = jnp.zeros(field.shape[:3] + (1,), jnp.float32)
    following = jnp.concatenate([field[..., 1:], zeros], axis=3)
    flux = coef * (following - field)
    flux_prev = jnp.concatenate([zeros, flux[..., :-1]], axis=3)
    return field + flux - flux_prev


def convective(field, convect_frac):
    column = jnp.mean(field, axis=1, keepdims=True)
    return field + convect_frac[None, None] * (column - field)


def reference(probe_signs, shift_cells, courant_frac, merid_coef, convect_frac, footprint, region_id, owner_slots, prior_slot):
    faces = merid_coef.at[:, NLAT - 1].set(0.0)
    probe = (2 * probe_signs - 1).astype(jnp.float32)
    adjoint = probe
    for turn in range(2):
        adjoint = zonal_adjoint(meridional(convective(adjoint, convect_frac), faces), courant_frac, shift_cells)
    bottom = footprint[None] * adjoint[:, 0]
    flat = bottom.reshape(TR, NLON * NLAT).T
    partial_value = jax.ops.segment_sum(flat, region_id.reshape(-1), num_segments=REGIONS).T
    sums = partial_value[:, owner_slots]
    scaled = prior_slot * sums
    by_region = jnp.zeros((TR, REGIONS), jnp.float32).at[:, owner_slots].set(scaled)
    surface = footprint[None] * by_region[:, region_id]
    source = jnp.concatenate([surface[:, None], jnp.zeros((TR, LEV - 1, NLON, NLAT), jnp.float32)], axis=1)
    for turn in range(2):
        source = convective(meridional(zonal_forward(source, courant_frac, shift_cells), faces), convect_frac)
    return probe * source
```

```python
import functools

import jax
import jax.numpy as jnp
from jax import lax
from jax.experimental import pallas as pl
from jax.experimental.pallas import tpu as pltpu
from jax.sharding import PartitionSpec as P

SUB, LANES = 8, 128


def swapped(block, axis, k):
    size = lax.axis_size(axis)
    return lax.ppermute(block, axis, [(i, i ^ k) for i in range(size)])


def transport_kernel(tracers, blocks, regions, own_ref, other_ref, owner_ref, prior_ref, out_ref, flat_ref):
    f32, i32 = jnp.float32, jnp.int32
    me = lax.axis_index("lon")
    place = [me ^ ((me + b) % blocks) if b else 0 for b in range(blocks)]
    bands = (own_ref, other_ref)
    cycle = blocks * SUB
    row = lax.broadcasted_iota(i32, (SUB, LANES), 0)
    lane = lax.broadcasted_iota(i32, (SUB, LANES), 1)
    first_row, last_row = row == 0, row == SUB - 1
    first_lane, last_lane = lane == 0, lane == LANES - 1
    base = tracers * 2 * SUB

    def tile(h, b, at):
        return bands[h][place[b], at : at + SUB, :]

    def full(h, at):
        return jnp.broadcast_to(bands[h][0, at : at + 1, :], (SUB, LANES))

    foot = [[tile(h, b, base) for h in range(2)] for b in range(blocks)]
    region = [[tile(h, b, base + SUB).astype(i32) for h in range(2)] for b in range(blocks)]
    half = [[0.5 * tile(h, b, base + 2 * SUB) for h in range(2)] for b in range(blocks)]
    at = base + 3 * SUB
    shift = [[full(h, at + l).astype(i32) for h in range(2)] for l in range(2)]
    frac = [[full(h, at + 2 + l) for h in range(2)] for l in range(2)]
    face = [[full(h, at + 4 + l) for h in range(2)] for l in range(2)]
    w_left = [[a * (a + 1.0) * 0.5 for a in x] for x in frac]
    w_centre = [[1.0 - a * a for a in x] for x in frac]
    w_right = [[a * (a - 1.0) * 0.5 for a in x] for x in frac]

    def north(v):
        r = [pltpu.roll(x, LANES - 1, 1) for x in v]
        return [jnp.where(last_lane, r[1], r[0]), jnp.where(last_lane, r[0], r[1])]

    def south(v):
        r = [pltpu.roll(x, 1, 1) for x in v]
        return [jnp.where(first_lane, r[1], r[0]), jnp.where(first_lane, r[0], r[1])]

    face_prev = [south(x) for x in face]
    face_mid = [[1.0 - face[l][h] - face_prev[l][h] for h in range(2)] for l in range(2)]

    def meridional(v, l, only=(0, 1)):
        n, s = north(v), south(v)
        return [face_mid[l][h] * v[h] + face[l][h] * n[h] + face_prev[l][h] * s[h] for h in only]

    def mod(e):
        return jnp.where(e >= blocks, e - blocks, e)

    steps = range((blocks - 1).bit_length())

    def bits(e):
        return [(e >> k) & 1 == 1 for k in steps]

    def plan(amount, ahead):
        whole, within = amount >> 3, amount & 7
        if ahead:
            crossed = (row < within).astype(i32)
            index = (row + within) & 7
        else:
            crossed = (row + within >= SUB).astype(i32)
            index = (row - within) & 7
        return bits(mod(mod(whole + crossed))), index

    def pick(v, plan, sign, wanted):
        masks, index = plan
        need = list(wanted)
        chain = []
        for k in reversed(steps):
            chain.append(need)
            need = sorted({(b + d) % blocks for b in need for d in (0, sign << k)})
        current = {b: v[b] for b in need}
        for k, need in zip(steps, reversed(chain)):
            current = {b: jnp.where(masks[k], current[(b + (sign << k)) % blocks], current[b]) for b in need}
        return [jnp.take_along_axis(current[b], index, axis=0, mode="promise_in_bounds") for b in wanted]

    def beside(v):
        up = [pltpu.roll(x, SUB - 1, 0) for x in v]
        down = [pltpu.roll(x, 1, 0) for x in v]
        after = [jnp.where(last_row, up[(b + 1) % blocks], up[b]) for b in range(blocks)]
        before = [jnp.where(first_row, down[(b - 1) % blocks], down[b]) for b in range(blocks)]
        return before, after

    every = range(blocks)
    plan_adjoint = [[plan(shift[l][h], True) for h in range(2)] for l in range(2)]
    plan_first = [plan(shift[0][h], False) for h in range(2)]
    plan_second = [
        [[plan(shift[l][h] + d, False) for d in (1, 0, -1)] for h in range(2)] for l in range(2)
    ]

    def zonal_adjoint(v, l):
        result = []
        for h in range(2):
            q = pick([v[b][h] for b in every], plan_adjoint[l][h], 1, every)
            before, after = beside(q)
            result.append(
                [w_left[l][h] * after[b] + w_centre[l][h] * q[b] + w_right[l][h] * before[b] for b in every]
            )
        return [[result[h][b] for h in range(2)] for b in every]

    for t in range(tracers):
        v = [[[tile(h, b, (2 * t + l) * SUB) for h in range(2)] for b in every] for l in range(2)]
        mixed = [[], []]
        for b in every:
            d = [half[b][h] * (v[1][b][h] - v[0][b][h]) for h in range(2)]
            mixed[0].append(meridional([v[0][b][h] + d[h] for h in range(2)], 0))
            mixed[1].append(meridional([v[1][b][h] - d[h] for h in range(2)], 1))
        v = [zonal_adjoint(mixed[l], l) for l in range(2)]
        mixed = [
            meridional([v[0][b][h] + half[b][h] * (v[1][b][h] - v[0][b][h]) for h in range(2)], 0) for b in every
        ]
        v = zonal_adjoint(mixed, 0)
        for b in every:
            for h in range(2):
                flat_ref[b, t * SUB : (t + 1) * SUB, h * LANES : (h + 1) * LANES] = foot[b][h] * v[b][h]

    bf16 = jnp.bfloat16
    lines = tracers * SUB
    total = jnp.zeros((3 * lines, SUB * regions), f32)
    number = lax.broadcasted_iota(i32, (1, regions, 2 * LANES), 1)
    for b in every:
        x = flat_ref[b]
        hi = x.astype(bf16)
        rest = x - hi.astype(f32)
        mid = rest.astype(bf16)
        low = (rest - mid.astype(f32)).astype(bf16)
        ids = jnp.concatenate(region[b], axis=1)
        same = ids[:, None, :] == number
        table = jnp.where(same, 1.0, 0.0).astype(bf16).reshape(SUB * regions, 2 * LANES)
        total = total + lax.dot_general(
            jnp.concatenate([hi, mid, low], axis=0),
            table,
            (((1,), (1,)), ((), ())),
            preferred_element_type=f32,
        )
    sums = total[:lines] + total[lines : 2 * lines] + total[2 * lines :]
    width = SUB * regions
    column = lax.broadcasted_iota(i32, (SUB, width), 1)
    keep = column // regions == lax.broadcasted_iota(i32, (SUB, width), 0)
    sums = jnp.concatenate(
        [
            jnp.sum(jnp.where(keep, sums[t * SUB : (t + 1) * SUB], 0.0), axis=0, keepdims=True)
            for t in range(tracers)
        ],
        axis=0,
    )
    while width > max(regions, LANES):
        width //= 2
        sums = sums[:, :width] + sums[:, width:]
    period = width
    while period > regions:
        period //= 2
        sums = sums + pltpu.roll(sums, period, 1)
    spot = lax.broadcasted_iota(i32, (width, regions), 0) % regions
    holds = jnp.where(spot == owner_ref[...], 1.0, 0.0)
    prior = lax.dot_general(
        prior_ref[...],
        holds,
        (((1,), (1,)), ((), ())),
        precision=lax.Precision.HIGHEST,
        preferred_element_type=f32,
    )
    scaled = sums * prior

    keep0 = [[1.0 - x for x in y] for y in half]
    for t in range(tracers):
        rows = jnp.broadcast_to(scaled[t : t + 1], (SUB, width))

        def spread(ids):
            result = None
            for k in range(width // LANES):
                part = jnp.take_along_axis(
                    rows[:, k * LANES : (k + 1) * LANES], ids & (LANES - 1), axis=1, mode="promise_in_bounds"
                )
                result = part if k == 0 else jnp.where(ids >> 7 == k, part, result)
            return result

        v = [[foot[b][h] * spread(region[b][h]) for h in range(2)] for b in every]
        u = []
        for h in range(2):
            p = pick([v[b][h] for b in every], plan_first[h], -1, every)
            before, after = beside(p)
            u.append(
                [w_left[0][h] * before[b] + w_centre[0][h] * p[b] + w_right[0][h] * after[b] for b in every]
            )
        u = [meridional([u[h][b] for h in range(2)], 0) for b in every]
        pair = [
            [[keep0[b][h] * u[b][h] for h in range(2)] for b in every],
            [[half[b][h] * u[b][h] for h in range(2)] for b in every],
        ]
        moved = []
        for l in range(2):
            z = []
            for h in range(2):
                source = [pair[l][b][h] for b in every]
                before, centre, after = (pick(source, p, -1, [0])[0] for p in plan_second[l][h])
                z.append(w_left[l][h] * before + w_centre[l][h] * centre + w_right[l][h] * after)
            moved.append(meridional(z, l, (0,))[0])
        d = half[0][0] * (moved[1] - moved[0])
        out_ref[t, 0] = tile(0, 0, 2 * t * SUB) * (moved[0] + d)
        out_ref[t, 1] = tile(0, 0, (2 * t + 1) * SUB) * (moved[1] - d)


def on_device(
    probe_signs,
    shift_cells,
    courant_frac,
    merid_coef,
    convect_frac,
    footprint,
    region_id,
    owner_slots,
    prior_slot,
):
    tracers, levels, width, rows = probe_signs.shape
    blocks, bands = lax.axis_size("lon"), lax.axis_size("lat")
    assert (levels, width, rows, bands) == (2, SUB, LANES, 2) and blocks & (blocks - 1) == 0
    regions = owner_slots.shape[0]
    f32 = jnp.float32
    at = lax.axis_index("lat") * rows + jnp.arange(rows, dtype=jnp.int32)
    faces = jnp.where((at == bands * rows - 1)[None, :], 0.0, merid_coef)
    block = jnp.concatenate(
        [
            (2 * probe_signs - 1).astype(f32).reshape(tracers * levels * width, rows),
            footprint,
            region_id.astype(f32),
            convect_frac,
            shift_cells.astype(f32),
            courant_frac,
            faces,
            jnp.zeros((2, rows), f32),
        ],
        axis=0,
    )
    own = jnp.stack([block] + [swapped(block, "lon", k) for k in range(1, blocks)])
    other = swapped(own, "lat", 1)
    return pl.pallas_call(
        functools.partial(transport_kernel, tracers, blocks, regions),
        out_shape=jax.ShapeDtypeStruct(probe_signs.shape, f32),
        in_specs=[pl.BlockSpec(memory_space=pltpu.VMEM)] * 4,
        out_specs=pl.BlockSpec(memory_space=pltpu.VMEM),
        scratch_shapes=[pltpu.VMEM((blocks, tracers * SUB, 2 * LANES), f32)],
        compiler_params=pltpu.CompilerParams(vmem_limit_bytes=48 * 1024 * 1024),
    )(own, other, owner_slots.reshape(1, regions), prior_slot)


def solution(mesh):
    placed = (
        P(("probe", "trc"), None, "lon", "lat"),
        P(None, "lat"),
        P(None, "lat"),
        P(None, "lat"),
        P("lon", "lat"),
        P("lon", "lat"),
        P("lon", "lat"),
        P(),
        P("trc", None),
    )
    return jax.shard_map(
        on_device,
        mesh=mesh,
        in_specs=placed,
        out_specs=P(("probe", "trc"), None, "lon", "lat"),
        check_vma=False,
    )
```

```python
import functools

import jax
import jax.numpy as jnp
from jax import lax
from jax.experimental import pallas as pl
from jax.experimental.pallas import tpu as pltpu
from jax.sharding import PartitionSpec as P

SUB, LANES = 8, 128


def swapped(block, axis, k):
    size = lax.axis_size(axis)
    return lax.ppermute(block, axis, [(i, i ^ k) for i in range(size)])


def slot_of(k, blocks):
    return jnp.where(k > 1, blocks + 1 - k, k)


def transport_kernel(tracers, blocks, regions, own_ref, other_ref, owner_ref, prior_ref, out_ref, flat_ref):
    f32, i32 = jnp.float32, jnp.int32
    me = lax.axis_index("lon")
    place = [slot_of(me ^ ((me + b) % blocks), blocks) if b else 0 for b in range(blocks)]
    bands = (own_ref, other_ref)
    cycle = blocks * SUB
    row = lax.broadcasted_iota(i32, (SUB, LANES), 0)
    lane = lax.broadcasted_iota(i32, (SUB, LANES), 1)
    first_row, last_row = row == 0, row == SUB - 1
    first_lane, last_lane = lane == 0, lane == LANES - 1
    base = tracers * 2 * SUB

    def tile(h, b, at):
        return bands[h][place[b], at : at + SUB, :]

    def full(h, at):
        return jnp.broadcast_to(bands[h][0, at : at + 1, :], (SUB, LANES))

    foot = [[tile(h, b, base) for h in range(2)] for b in range(blocks)]
    region = [[tile(h, b, base + SUB).astype(i32) for h in range(2)] for b in range(blocks)]
    half = [[0.5 * tile(h, b, base + 2 * SUB) for h in range(2)] for b in range(blocks)]
    at = base + 3 * SUB
    shift = [[full(h, at + l).astype(i32) for h in range(2)] for l in range(2)]
    frac = [[full(h, at + 2 + l) for h in range(2)] for l in range(2)]
    face = [[full(h, at + 4 + l) for h in range(2)] for l in range(2)]
    w_left = [[a * (a + 1.0) * 0.5 for a in x] for x in frac]
    w_centre = [[1.0 - a * a for a in x] for x in frac]
    w_right = [[a * (a - 1.0) * 0.5 for a in x] for x in frac]

    def north(v):
        r = [pltpu.roll(x, LANES - 1, 1) for x in v]
        return [jnp.where(last_lane, r[1], r[0]), jnp.where(last_lane, r[0], r[1])]

    def south(v):
        r = [pltpu.roll(x, 1, 1) for x in v]
        return [jnp.where(first_lane, r[1], r[0]), jnp.where(first_lane, r[0], r[1])]

    face_prev = [south(x) for x in face]
    face_mid = [[1.0 - face[l][h] - face_prev[l][h] for h in range(2)] for l in range(2)]

    def meridional(v, l, only=(0, 1)):
        n, s = north(v), south(v)
        return [face_mid[l][h] * v[h] + face[l][h] * n[h] + face_prev[l][h] * s[h] for h in only]

    def mod(e):
        return jnp.where(e >= blocks, e - blocks, e)

    steps = range((blocks - 1).bit_length())

    def bits(e):
        return [(e >> k) & 1 == 1 for k in steps]

    def plan(amount, ahead):
        whole, within = amount >> 3, amount & 7
        if ahead:
            crossed = (row < within).astype(i32)
            index = (row + within) & 7
        else:
            crossed = (row + within >= SUB).astype(i32)
            index = (row - within) & 7
        return bits(mod(mod(whole + crossed))), index

    def pick(v, plan, sign, wanted):
        masks, index = plan
        need = list(wanted)
        chain = []
        for k in reversed(steps):
            chain.append(need)
            need = sorted({(b + d) % blocks for b in need for d in (0, sign << k)})
        current = {b: v[b] for b in need}
        for k, need in zip(steps, reversed(chain)):
            current = {b: jnp.where(masks[k], current[(b + (sign << k)) % blocks], current[b]) for b in need}
        return [jnp.take_along_axis(current[b], index, axis=0, mode="promise_in_bounds") for b in wanted]

    def beside(v):
        up = [pltpu.roll(x, SUB - 1, 0) for x in v]
        down = [pltpu.roll(x, 1, 0) for x in v]
        after = [jnp.where(last_row, up[(b + 1) % blocks], up[b]) for b in range(blocks)]
        before = [jnp.where(first_row, down[(b - 1) % blocks], down[b]) for b in range(blocks)]
        return before, after

    every = range(blocks)
    plan_adjoint = [[plan(shift[l][h], True) for h in range(2)] for l in range(2)]
    plan_first = [plan(shift[0][h], False) for h in range(2)]
    plan_second = [
        [[plan(shift[l][h] + d, False) for d in (1, 0, -1)] for h in range(2)] for l in range(2)
    ]

    def zonal_adjoint(v, l):
        result = []
        for h in range(2):
            q = pick([v[b][h] for b in every], plan_adjoint[l][h], 1, every)
            before, after = beside(q)
            result.append(
                [w_left[l][h] * after[b] + w_centre[l][h] * q[b] + w_right[l][h] * before[b] for b in every]
            )
        return [[result[h][b] for h in range(2)] for b in every]

    for t in range(tracers):
        v = [[[tile(h, b, (2 * t + l) * SUB) for h in range(2)] for b in every] for l in range(2)]
        mixed = [[], []]
        for b in every:
            d = [half[b][h] * (v[1][b][h] - v[0][b][h]) for h in range(2)]
            mixed[0].append(meridional([v[0][b][h] + d[h] for h in range(2)], 0))
            mixed[1].append(meridional([v[1][b][h] - d[h] for h in range(2)], 1))
        v = [zonal_adjoint(mixed[l], l) for l in range(2)]
        mixed = [
            meridional([v[0][b][h] + half[b][h] * (v[1][b][h] - v[0][b][h]) for h in range(2)], 0) for b in every
        ]
        v = zonal_adjoint(mixed, 0)
        for b in every:
            for h in range(2):
                flat_ref[b, t * SUB : (t + 1) * SUB, h * LANES : (h + 1) * LANES] = foot[b][h] * v[b][h]

    bf16 = jnp.bfloat16
    lines = tracers * SUB
    total = jnp.zeros((3 * lines, SUB * regions), f32)
    number = lax.broadcasted_iota(i32, (1, regions, 2 * LANES), 1)
    for b in every:
        x = flat_ref[b]
        hi = x.astype(bf16)
        rest = x - hi.astype(f32)
        mid = rest.astype(bf16)
        low = (rest - mid.astype(f32)).astype(bf16)
        ids = jnp.concatenate(region[b], axis=1)
        same = ids[:, None, :] == number
        table = jnp.where(same, 1.0, 0.0).astype(bf16).reshape(SUB * regions, 2 * LANES)
        total = total + lax.dot_general(
            jnp.concatenate([hi, mid, low], axis=0),
            table,
            (((1,), (1,)), ((), ())),
            preferred_element_type=f32,
        )
    sums = total[:lines] + total[lines : 2 * lines] + total[2 * lines :]
    width = SUB * regions
    column = lax.broadcasted_iota(i32, (SUB, width), 1)
    keep = column // regions == lax.broadcasted_iota(i32, (SUB, width), 0)
    sums = jnp.concatenate(
        [
            jnp.sum(jnp.where(keep, sums[t * SUB : (t + 1) * SUB], 0.0), axis=0, keepdims=True)
            for t in range(tracers)
        ],
        axis=0,
    )
    while width > max(regions, LANES):
        width //= 2
        sums = sums[:, :width] + sums[:, width:]
    period = width
    while period > regions:
        period //= 2
        sums = sums + pltpu.roll(sums, period, 1)
    spot = lax.broadcasted_iota(i32, (width, regions), 0) % regions
    holds = jnp.where(spot == owner_ref[...], 1.0, 0.0)
    prior = lax.dot_general(
        prior_ref[...],
        holds,
        (((1,), (1,)), ((), ())),
        precision=lax.Precision.HIGHEST,
        preferred_element_type=f32,
    )
    scaled = sums * prior

    keep0 = [[1.0 - x for x in y] for y in half]
    for t in range(tracers):
        rows = jnp.broadcast_to(scaled[t : t + 1], (SUB, width))

        def spread(ids):
            result = None
            for k in range(width // LANES):
                part = jnp.take_along_axis(
                    rows[:, k * LANES : (k + 1) * LANES], ids & (LANES - 1), axis=1, mode="promise_in_bounds"
                )
                result = part if k == 0 else jnp.where(ids >> 7 == k, part, result)
            return result

        v = [[foot[b][h] * spread(region[b][h]) for h in range(2)] for b in every]
        u = []
        for h in range(2):
            p = pick([v[b][h] for b in every], plan_first[h], -1, every)
            before, after = beside(p)
            u.append(
                [w_left[0][h] * before[b] + w_centre[0][h] * p[b] + w_right[0][h] * after[b] for b in every]
            )
        u = [meridional([u[h][b] for h in range(2)], 0) for b in every]
        pair = [
            [[keep0[b][h] * u[b][h] for h in range(2)] for b in every],
            [[half[b][h] * u[b][h] for h in range(2)] for b in every],
        ]
        moved = []
        for l in range(2):
            z = []
            for h in range(2):
                source = [pair[l][b][h] for b in every]
                before, centre, after = (pick(source, p, -1, [0])[0] for p in plan_second[l][h])
                z.append(w_left[l][h] * before + w_centre[l][h] * centre + w_right[l][h] * after)
            moved.append(meridional(z, l, (0,))[0])
        d = half[0][0] * (moved[1] - moved[0])
        out_ref[t, 0] = tile(0, 0, 2 * t * SUB) * (moved[0] + d)
        out_ref[t, 1] = tile(0, 0, (2 * t + 1) * SUB) * (moved[1] - d)


def pack_kernel(tracers, sign_ref, shift_ref, frac_ref, face_ref, convect_ref, foot_ref, region_ref, out_ref, *scratch):
    f32, i32 = jnp.float32, jnp.int32
    sources = (sign_ref, foot_ref, region_ref, convect_ref, shift_ref, frac_ref, face_ref)
    held, arrived = scratch[:-1], scratch[-1]
    copies = [
        pltpu.make_async_copy(source, slot, arrived.at[n])
        for n, (source, slot) in enumerate(zip(sources, held))
    ]
    for copy in copies:
        copy.start()
    signs, foot, region, convect, shift, frac, face = held
    base = tracers * 2 * SUB
    for n, slot in ((1, foot), (2, region), (3, convect)):
        copies[n].wait()
        out_ref[base + (n - 1) * SUB : base + n * SUB, :] = slot[...].astype(f32)
    for n in (4, 5, 6):
        copies[n].wait()
    ends = lax.axis_index("lat") == lax.axis_size("lat") - 1
    lane = lax.broadcasted_iota(i32, (2, LANES), 1)
    closed = jnp.where(ends, LANES - 1, LANES)
    out_ref[base + 3 * SUB : base + 4 * SUB, :] = jnp.concatenate(
        [
            shift[...].astype(f32),
            frac[...],
            jnp.where(lane == closed, 0.0, face[...]),
            jnp.zeros((2, LANES), f32),
        ],
        axis=0,
    )
    copies[0].wait()
    for t in range(tracers):
        for l in range(2):
            out_ref[(2 * t + l) * SUB : (2 * t + l + 1) * SUB, :] = (2 * signs[t, l] - 1).astype(f32)


def on_device(
    probe_signs,
    shift_cells,
    courant_frac,
    merid_coef,
    convect_frac,
    footprint,
    region_id,
    owner_slots,
    prior_slot,
):
    tracers, levels, width, rows = probe_signs.shape
    blocks, bands = lax.axis_size("lon"), lax.axis_size("lat")
    assert (levels, width, rows, bands) == (2, SUB, LANES, 2) and blocks & (blocks - 1) == 0
    regions = owner_slots.shape[0]
    f32 = jnp.float32
    anywhere = pl.BlockSpec(memory_space=pl.ANY)
    fields = (probe_signs, footprint, region_id, convect_frac, shift_cells, courant_frac, merid_coef)
    block = pl.pallas_call(
        functools.partial(pack_kernel, tracers),
        out_shape=pltpu.VMEM((tracers * levels * width + 4 * SUB, rows), f32),
        in_specs=[anywhere] * 7,
        out_specs=pl.BlockSpec(memory_space=pltpu.VMEM),
        scratch_shapes=[pltpu.VMEM(x.shape, x.dtype) for x in fields] + [pltpu.SemaphoreType.DMA((7,))],
    )(probe_signs, shift_cells, courant_frac, merid_coef, convect_frac, footprint, region_id)
    order = sorted(range(1, blocks), key=lambda k: (k > 1, -k))
    own = jnp.stack([block] + [swapped(block, "lon", k) for k in order])
    other = swapped(own, "lat", 1)
    return pl.pallas_call(
        functools.partial(transport_kernel, tracers, blocks, regions),
        out_shape=jax.ShapeDtypeStruct(probe_signs.shape, f32),
        in_specs=[pl.BlockSpec(memory_space=pltpu.VMEM)] * 4,
        out_specs=pl.BlockSpec(memory_space=pltpu.VMEM),
        scratch_shapes=[pltpu.VMEM((blocks, tracers * SUB, 2 * LANES), f32)],
        compiler_params=pltpu.CompilerParams(vmem_limit_bytes=48 * 1024 * 1024),
    )(own, other, owner_slots.reshape(1, regions), prior_slot)


def solution(mesh):
    placed = (
        P(("probe", "trc"), None, "lon", "lat"),
        P(None, "lat"),
        P(None, "lat"),
        P(None, "lat"),
        P("lon", "lat"),
        P("lon", "lat"),
        P("lon", "lat"),
        P(),
        P("trc", None),
    )
    return jax.shard_map(
        on_device,
        mesh=mesh,
        in_specs=placed,
        out_specs=P(("probe", "trc"), None, "lon", "lat"),
        check_vma=False,
    )
```

```python
import functools

import jax
import jax.numpy as jnp
from jax import lax
from jax.experimental import pallas as pl
from jax.experimental.pallas import tpu as pltpu
from jax.sharding import PartitionSpec as P

SUB, LANES = 8, 128


def swapped(block, axis, k):
    size = lax.axis_size(axis)
    return lax.ppermute(block, axis, [(i, i ^ k) for i in range(size)])


def slot_of(k, blocks):
    return jnp.where(k > 1, k - 1, k * (blocks - 1))


def transport_kernel(tracers, blocks, regions, own_ref, other_ref, owner_ref, prior_ref, out_ref, flat_ref):
    f32, i32 = jnp.float32, jnp.int32
    me = lax.axis_index("lon")
    place = [slot_of(me ^ ((me + b) % blocks), blocks) if b else 0 for b in range(blocks)]
    bands = (own_ref, other_ref)
    cycle = blocks * SUB
    row = lax.broadcasted_iota(i32, (SUB, LANES), 0)
    lane = lax.broadcasted_iota(i32, (SUB, LANES), 1)
    first_row, last_row = row == 0, row == SUB - 1
    first_lane, last_lane = lane == 0, lane == LANES - 1
    base = tracers * 2 * SUB
    stride = base + 3 * SUB

    def tile(h, b, at):
        return bands[h][pl.ds(pl.multiple_of(place[b] * stride, SUB) + at, SUB), :]

    def full(h, at):
        return jnp.broadcast_to(bands[h][at : at + 1, :], (SUB, LANES))

    foot = [[tile(h, b, base) for h in range(2)] for b in range(blocks)]
    region = [[tile(h, b, base + SUB).astype(i32) for h in range(2)] for b in range(blocks)]
    half = [[tile(h, b, base + 2 * SUB) for h in range(2)] for b in range(blocks)]
    at = blocks * stride
    shift = [[full(h, at + l).astype(i32) for h in range(2)] for l in range(2)]
    face, w_left, w_centre, w_right = (
        [[full(h, at + 2 * n + l) for h in range(2)] for l in range(2)] for n in range(1, 5)
    )

    def north(v):
        r = [pltpu.roll(x, LANES - 1, 1) for x in v]
        return [jnp.where(last_lane, r[1], r[0]), jnp.where(last_lane, r[0], r[1])]

    def south(v):
        r = [pltpu.roll(x, 1, 1) for x in v]
        return [jnp.where(first_lane, r[1], r[0]), jnp.where(first_lane, r[0], r[1])]

    face_prev = [south(x) for x in face]
    face_mid = [[1.0 - face[l][h] - face_prev[l][h] for h in range(2)] for l in range(2)]

    def meridional(v, l, only=(0, 1)):
        n, s = north(v), south(v)
        return [face_mid[l][h] * v[h] + face[l][h] * n[h] + face_prev[l][h] * s[h] for h in only]

    steps = range((blocks - 1).bit_length())

    def bits(e):
        return [e & (1 << k) != 0 for k in steps]

    def plan(amount, ahead):
        whole, within = amount >> 3, amount & 7
        if ahead:
            crossed = (row < within).astype(i32)
            index = (row + within) & 7
        else:
            crossed = (row + within >= SUB).astype(i32)
            index = (row - within) & 7
        return bits(whole + crossed), index

    def pick(v, plan, sign, wanted):
        masks, index = plan
        need = list(wanted)
        chain = []
        for k in reversed(steps):
            chain.append(need)
            need = sorted({(b + d) % blocks for b in need for d in (0, sign << k)})
        current = {b: v[b] for b in need}
        for k, need in zip(steps, reversed(chain)):
            current = {b: jnp.where(masks[k], current[(b + (sign << k)) % blocks], current[b]) for b in need}
        return [jnp.take_along_axis(current[b], index, axis=0, mode="promise_in_bounds") for b in wanted]

    def beside(v):
        after = [pltpu.roll(jnp.where(first_row, v[(b + 1) % blocks], v[b]), SUB - 1, 0) for b in range(blocks)]
        before = [pltpu.roll(jnp.where(last_row, v[(b - 1) % blocks], v[b]), 1, 0) for b in range(blocks)]
        return before, after

    every = range(blocks)
    plan_adjoint = [[plan(shift[l][h], True) for h in range(2)] for l in range(2)]
    plan_first = [plan(shift[0][h], False) for h in range(2)]
    plan_second = [
        [[plan(shift[l][h] + d, False) for d in (1, 0, -1)] for h in range(2)] for l in range(2)
    ]

    def zonal_adjoint(v, l):
        result = []
        for h in range(2):
            q = pick([v[b][h] for b in every], plan_adjoint[l][h], 1, every)
            before, after = beside(q)
            result.append(
                [w_left[l][h] * after[b] + w_centre[l][h] * q[b] + w_right[l][h] * before[b] for b in every]
            )
        return [[result[h][b] for h in range(2)] for b in every]

    for t in range(tracers):
        v = [[[tile(h, b, (2 * t + l) * SUB) for h in range(2)] for b in every] for l in range(2)]
        mixed = [[], []]
        for b in every:
            d = [half[b][h] * (v[1][b][h] - v[0][b][h]) for h in range(2)]
            mixed[0].append(meridional([v[0][b][h] + d[h] for h in range(2)], 0))
            mixed[1].append(meridional([v[1][b][h] - d[h] for h in range(2)], 1))
        v = [zonal_adjoint(mixed[l], l) for l in range(2)]
        mixed = [
            meridional([v[0][b][h] + half[b][h] * (v[1][b][h] - v[0][b][h]) for h in range(2)], 0) for b in every
        ]
        v = zonal_adjoint(mixed, 0)
        for b in every:
            for h in range(2):
                flat_ref[b, t * SUB : (t + 1) * SUB, h * LANES : (h + 1) * LANES] = foot[b][h] * v[b][h]

    bf16 = jnp.bfloat16
    lines = tracers * SUB
    total = jnp.zeros((3 * lines, SUB * regions), f32)
    number = lax.broadcasted_iota(i32, (regions, 2 * LANES), 0).astype(bf16)[None]
    for b in every:
        x = flat_ref[b]
        hi = x.astype(bf16)
        rest = x - hi.astype(f32)
        mid = rest.astype(bf16)
        low = (rest - mid.astype(f32)).astype(bf16)
        ids = jnp.concatenate(region[b], axis=1).astype(f32)
        ids = jnp.broadcast_to(ids[:, None, :], (SUB, regions, 2 * LANES)).astype(bf16)
        one, zero = jnp.ones((), bf16), jnp.zeros((), bf16)
        table = jnp.where(ids == number, one, zero).reshape(SUB * regions, 2 * LANES)
        total = total + lax.dot_general(
            jnp.concatenate([hi, mid, low], axis=0),
            table,
            (((1,), (1,)), ((), ())),
            preferred_element_type=f32,
        )
    sums = total[:lines] + total[lines : 2 * lines] + total[2 * lines :]
    width = SUB * regions
    column = lax.broadcasted_iota(i32, (SUB, width), 1)
    keep = column // regions == lax.broadcasted_iota(i32, (SUB, width), 0)
    sums = jnp.concatenate(
        [
            jnp.sum(jnp.where(keep, sums[t * SUB : (t + 1) * SUB], 0.0), axis=0, keepdims=True)
            for t in range(tracers)
        ],
        axis=0,
    )
    while width > max(regions, LANES):
        width //= 2
        sums = sums[:, :width] + sums[:, width:]
    period = width
    while period > regions:
        period //= 2
        sums = sums + pltpu.roll(sums, period, 1)
    spot = lax.broadcasted_iota(i32, (width, regions), 0) % regions
    holds = jnp.where(spot == owner_ref[...], 1.0, 0.0)
    prior = lax.dot_general(
        prior_ref[...],
        holds,
        (((1,), (1,)), ((), ())),
        precision=lax.Precision.HIGHEST,
        preferred_element_type=f32,
    )
    scaled = sums * prior

    keep0 = [[1.0 - x for x in y] for y in half]
    for t in range(tracers):
        rows = jnp.broadcast_to(scaled[t : t + 1], (SUB, width))

        def spread(ids):
            result = None
            for k in range(width // LANES):
                part = jnp.take_along_axis(
                    rows[:, k * LANES : (k + 1) * LANES], ids & (LANES - 1), axis=1, mode="promise_in_bounds"
                )
                result = part if k == 0 else jnp.where(ids >> 7 == k, part, result)
            return result

        v = [[foot[b][h] * spread(region[b][h]) for h in range(2)] for b in every]
        u = []
        for h in range(2):
            p = pick([v[b][h] for b in every], plan_first[h], -1, every)
            before, after = beside(p)
            u.append(
                [w_left[0][h] * before[b] + w_centre[0][h] * p[b] + w_right[0][h] * after[b] for b in every]
            )
        u = [meridional([u[h][b] for h in range(2)], 0) for b in every]
        pair = [
            [[keep0[b][h] * u[b][h] for h in range(2)] for b in every],
            [[half[b][h] * u[b][h] for h in range(2)] for b in every],
        ]
        moved = []
        for l in range(2):
            z = []
            for h in range(2):
                source = [pair[l][b][h] for b in every]
                before, centre, after = (pick(source, p, -1, [0])[0] for p in plan_second[l][h])
                z.append(w_left[l][h] * before + w_centre[l][h] * centre + w_right[l][h] * after)
            moved.append(meridional(z, l, (0,))[0])
        d = half[0][0] * (moved[1] - moved[0])
        out_ref[t, 0] = tile(0, 0, 2 * t * SUB) * (moved[0] + d)
        out_ref[t, 1] = tile(0, 0, (2 * t + 1) * SUB) * (moved[1] - d)


def pack_kernel(tracers, sign_ref, shift_ref, frac_ref, face_ref, convect_ref, foot_ref, region_ref, out_ref, rows_ref, *scratch):
    f32, i32 = jnp.float32, jnp.int32
    sources = (sign_ref, foot_ref, region_ref, convect_ref, shift_ref, frac_ref, face_ref)
    held, arrived = scratch[:-1], scratch[-1]
    copies = [
        pltpu.make_async_copy(source, slot, arrived.at[n])
        for n, (source, slot) in enumerate(zip(sources, held))
    ]
    for copy in copies:
        copy.start()
    signs, foot, region, convect, shift, frac, face = held
    base = tracers * 2 * SUB
    for n, slot in ((1, foot), (2, region), (3, convect)):
        copies[n].wait()
        value = slot[...].astype(f32)
        out_ref[base + (n - 1) * SUB : base + n * SUB, :] = 0.5 * value if n == 3 else value
    for n in (4, 5, 6):
        copies[n].wait()
    ends = lax.axis_index("lat") == lax.axis_size("lat") - 1
    lane = lax.broadcasted_iota(i32, (2, LANES), 1)
    closed = jnp.where(ends, LANES - 1, LANES)
    a = frac[...]
    rows_ref[...] = jnp.concatenate(
        [
            shift[...].astype(f32),
            jnp.where(lane == closed, 0.0, face[...]),
            a * (a + 1.0) * 0.5,
            1.0 - a * a,
            a * (a - 1.0) * 0.5,
            jnp.zeros((6, LANES), f32),
        ],
        axis=0,
    )
    copies[0].wait()
    for t in range(tracers):
        for l in range(2):
            out_ref[(2 * t + l) * SUB : (2 * t + l + 1) * SUB, :] = (2 * signs[t, l] - 1).astype(f32)


def on_device(
    probe_signs,
    shift_cells,
    courant_frac,
    merid_coef,
    convect_frac,
    footprint,
    region_id,
    owner_slots,
    prior_slot,
):
    tracers, levels, width, rows = probe_signs.shape
    blocks, bands = lax.axis_size("lon"), lax.axis_size("lat")
    assert (levels, width, rows, bands) == (2, SUB, LANES, 2) and blocks & (blocks - 1) == 0
    regions = owner_slots.shape[0]
    f32 = jnp.float32
    anywhere = pl.BlockSpec(memory_space=pl.ANY)
    fields = (probe_signs, footprint, region_id, convect_frac, shift_cells, courant_frac, merid_coef)
    block, params = pl.pallas_call(
        functools.partial(pack_kernel, tracers),
        out_shape=(pltpu.VMEM((tracers * levels * width + 3 * SUB, rows), f32), pltpu.VMEM((2 * SUB, rows), f32)),
        in_specs=[anywhere] * 7,
        out_specs=[pl.BlockSpec(memory_space=pltpu.VMEM)] * 2,
        scratch_shapes=[pltpu.VMEM(x.shape, x.dtype) for x in fields] + [pltpu.SemaphoreType.DMA((7,))],
    )(probe_signs, shift_cells, courant_frac, merid_coef, convect_frac, footprint, region_id)
    order = [*range(2, blocks), 1]
    own = jnp.concatenate([block] + [swapped(block, "lon", k) for k in order] + [params])
    other = swapped(own, "lat", 1)
    return pl.pallas_call(
        functools.partial(transport_kernel, tracers, blocks, regions),
        out_shape=jax.ShapeDtypeStruct(probe_signs.shape, f32),
        in_specs=[pl.BlockSpec(memory_space=pltpu.VMEM)] * 4,
        out_specs=pl.BlockSpec(memory_space=pltpu.VMEM),
        scratch_shapes=[pltpu.VMEM((blocks, tracers * SUB, 2 * LANES), f32)],
        compiler_params=pltpu.CompilerParams(vmem_limit_bytes=48 * 1024 * 1024),
    )(own, other, owner_slots.reshape(1, regions), prior_slot)


def solution(mesh):
    placed = (
        P(("probe", "trc"), None, "lon", "lat"),
        P(None, "lat"),
        P(None, "lat"),
        P(None, "lat"),
        P("lon", "lat"),
        P("lon", "lat"),
        P("lon", "lat"),
        P(),
        P("trc", None),
    )
    return jax.shard_map(
        on_device,
        mesh=mesh,
        in_specs=placed,
        out_specs=P(("probe", "trc"), None, "lon", "lat"),
        check_vma=False,
    )
```

```python
import functools

import jax
import jax.numpy as jnp
from jax import lax
from jax.experimental import pallas as pl
from jax.experimental.pallas import tpu as pltpu
from jax.sharding import PartitionSpec as P

SUB, LANES = 8, 128


def swapped(block, axis, k):
    size = lax.axis_size(axis)
    return lax.ppermute(block, axis, [(i, i ^ k) for i in range(size)])


def ring(i):
    return i ^ (i >> 1)


def turned(block, k):
    size = lax.axis_size("lon")
    spot = {ring(i): i for i in range(size)}
    return lax.ppermute(block, "lon", [(i, spot[(ring(i) + k) % size]) for i in range(size)])


def transport_kernel(tracers, blocks, regions, own_ref, other_ref, owner_ref, prior_ref, out_ref, flat_ref):
    f32, i32 = jnp.float32, jnp.int32
    me = lax.axis_index("lon")
    place = [(ring(me) - ring((me + b) % blocks)) % blocks if b else 0 for b in range(blocks)]
    bands = (own_ref, other_ref)
    cycle = blocks * SUB
    row = lax.broadcasted_iota(i32, (SUB, LANES), 0)
    lane = lax.broadcasted_iota(i32, (SUB, LANES), 1)
    first_row, last_row = row == 0, row == SUB - 1
    first_lane, last_lane = lane == 0, lane == LANES - 1
    base = tracers * 2 * SUB
    stride = base + 3 * SUB

    def tile(h, b, at):
        return bands[h][pl.ds(pl.multiple_of(place[b] * stride, SUB) + at, SUB), :]

    def full(h, at):
        return jnp.broadcast_to(bands[h][at : at + 1, :], (SUB, LANES))

    foot = [[tile(h, b, base) for h in range(2)] for b in range(blocks)]
    region = [[tile(h, b, base + SUB).astype(i32) for h in range(2)] for b in range(blocks)]
    half = [[tile(h, b, base + 2 * SUB) for h in range(2)] for b in range(blocks)]
    at = blocks * stride
    shift = [[full(h, at + l).astype(i32) for h in range(2)] for l in range(2)]
    face, w_left, w_centre, w_right = (
        [[full(h, at + 2 * n + l) for h in range(2)] for l in range(2)] for n in range(1, 5)
    )

    def north(v):
        r = [pltpu.roll(x, LANES - 1, 1) for x in v]
        return [jnp.where(last_lane, r[1], r[0]), jnp.where(last_lane, r[0], r[1])]

    def south(v):
        r = [pltpu.roll(x, 1, 1) for x in v]
        return [jnp.where(first_lane, r[1], r[0]), jnp.where(first_lane, r[0], r[1])]

    face_prev = [south(x) for x in face]
    face_mid = [[1.0 - face[l][h] - face_prev[l][h] for h in range(2)] for l in range(2)]

    def meridional(v, l, only=(0, 1)):
        n, s = north(v), south(v)
        return [face_mid[l][h] * v[h] + face[l][h] * n[h] + face_prev[l][h] * s[h] for h in only]

    steps = range((blocks - 1).bit_length())

    def bits(e):
        return [e & (1 << k) != 0 for k in steps]

    def plan(amount, ahead):
        whole, within = amount >> 3, amount & 7
        if ahead:
            crossed = (row < within).astype(i32)
            index = (row + within) & 7
        else:
            crossed = (row + within >= SUB).astype(i32)
            index = (row - within) & 7
        return bits(whole + crossed), index

    def pick(v, plan, sign, wanted):
        masks, index = plan
        need = list(wanted)
        chain = []
        for k in reversed(steps):
            chain.append(need)
            need = sorted({(b + d) % blocks for b in need for d in (0, sign << k)})
        current = {b: v[b] for b in need}
        for k, need in zip(steps, reversed(chain)):
            current = {b: jnp.where(masks[k], current[(b + (sign << k)) % blocks], current[b]) for b in need}
        return [jnp.take_along_axis(current[b], index, axis=0, mode="promise_in_bounds") for b in wanted]

    def beside(v):
        after = [pltpu.roll(jnp.where(first_row, v[(b + 1) % blocks], v[b]), SUB - 1, 0) for b in range(blocks)]
        before = [pltpu.roll(jnp.where(last_row, v[(b - 1) % blocks], v[b]), 1, 0) for b in range(blocks)]
        return before, after

    every = range(blocks)
    plan_adjoint = [[plan(shift[l][h], True) for h in range(2)] for l in range(2)]
    plan_first = [plan(shift[0][h], False) for h in range(2)]
    plan_second = [
        [[plan(shift[l][h] + d, False) for d in (1, 0, -1)] for h in range(2)] for l in range(2)
    ]

    def zonal_adjoint(v, l):
        result = []
        for h in range(2):
            q = pick([v[b][h] for b in every], plan_adjoint[l][h], 1, every)
            before, after = beside(q)
            result.append(
                [w_left[l][h] * after[b] + w_centre[l][h] * q[b] + w_right[l][h] * before[b] for b in every]
            )
        return [[result[h][b] for h in range(2)] for b in every]

    for t in range(tracers):
        v = [[[tile(h, b, (2 * t + l) * SUB) for h in range(2)] for b in every] for l in range(2)]
        mixed = [[], []]
        for b in every:
            d = [half[b][h] * (v[1][b][h] - v[0][b][h]) for h in range(2)]
            mixed[0].append(meridional([v[0][b][h] + d[h] for h in range(2)], 0))
            mixed[1].append(meridional([v[1][b][h] - d[h] for h in range(2)], 1))
        v = [zonal_adjoint(mixed[l], l) for l in range(2)]
        mixed = [
            meridional([v[0][b][h] + half[b][h] * (v[1][b][h] - v[0][b][h]) for h in range(2)], 0) for b in every
        ]
        v = zonal_adjoint(mixed, 0)
        for b in every:
            for h in range(2):
                flat_ref[b, t * SUB : (t + 1) * SUB, h * LANES : (h + 1) * LANES] = foot[b][h] * v[b][h]

    bf16 = jnp.bfloat16
    lines = tracers * SUB
    total = jnp.zeros((3 * lines, SUB * regions), f32)
    number = lax.broadcasted_iota(i32, (regions, 2 * LANES), 0).astype(bf16)[None]
    for b in every:
        x = flat_ref[b]
        hi = x.astype(bf16)
        rest = x - hi.astype(f32)
        mid = rest.astype(bf16)
        low = (rest - mid.astype(f32)).astype(bf16)
        ids = jnp.concatenate(region[b], axis=1).astype(f32)
        ids = jnp.broadcast_to(ids[:, None, :], (SUB, regions, 2 * LANES)).astype(bf16)
        one, zero = jnp.ones((), bf16), jnp.zeros((), bf16)
        table = jnp.where(ids == number, one, zero).reshape(SUB * regions, 2 * LANES)
        total = total + lax.dot_general(
            jnp.concatenate([hi, mid, low], axis=0),
            table,
            (((1,), (1,)), ((), ())),
            preferred_element_type=f32,
        )
    sums = total[:lines] + total[lines : 2 * lines] + total[2 * lines :]
    width = SUB * regions
    column = lax.broadcasted_iota(i32, (SUB, width), 1)
    keep = column // regions == lax.broadcasted_iota(i32, (SUB, width), 0)
    sums = jnp.concatenate(
        [
            jnp.sum(jnp.where(keep, sums[t * SUB : (t + 1) * SUB], 0.0), axis=0, keepdims=True)
            for t in range(tracers)
        ],
        axis=0,
    )
    while width > max(regions, LANES):
        width //= 2
        sums = sums[:, :width] + sums[:, width:]
    period = width
    while period > regions:
        period //= 2
        sums = sums + pltpu.roll(sums, period, 1)
    spot = lax.broadcasted_iota(i32, (width, regions), 0) % regions
    holds = jnp.where(spot == owner_ref[...], 1.0, 0.0)
    prior = lax.dot_general(
        prior_ref[...],
        holds,
        (((1,), (1,)), ((), ())),
        precision=lax.Precision.HIGHEST,
        preferred_element_type=f32,
    )
    scaled = sums * prior

    keep0 = [[1.0 - x for x in y] for y in half]
    for t in range(tracers):
        rows = jnp.broadcast_to(scaled[t : t + 1], (SUB, width))

        def spread(ids):
            result = None
            for k in range(width // LANES):
                part = jnp.take_along_axis(
                    rows[:, k * LANES : (k + 1) * LANES], ids & (LANES - 1), axis=1, mode="promise_in_bounds"
                )
                result = part if k == 0 else jnp.where(ids >> 7 == k, part, result)
            return result

        v = [[foot[b][h] * spread(region[b][h]) for h in range(2)] for b in every]
        u = []
        for h in range(2):
            p = pick([v[b][h] for b in every], plan_first[h], -1, every)
            before, after = beside(p)
            u.append(
                [w_left[0][h] * before[b] + w_centre[0][h] * p[b] + w_right[0][h] * after[b] for b in every]
            )
        u = [meridional([u[h][b] for h in range(2)], 0) for b in every]
        pair = [
            [[keep0[b][h] * u[b][h] for h in range(2)] for b in every],
            [[half[b][h] * u[b][h] for h in range(2)] for b in every],
        ]
        moved = []
        for l in range(2):
            z = []
            for h in range(2):
                source = [pair[l][b][h] for b in every]
                before, centre, after = (pick(source, p, -1, [0])[0] for p in plan_second[l][h])
                z.append(w_left[l][h] * before + w_centre[l][h] * centre + w_right[l][h] * after)
            moved.append(meridional(z, l, (0,))[0])
        d = half[0][0] * (moved[1] - moved[0])
        out_ref[t, 0] = tile(0, 0, 2 * t * SUB) * (moved[0] + d)
        out_ref[t, 1] = tile(0, 0, (2 * t + 1) * SUB) * (moved[1] - d)


def pack_kernel(tracers, sign_ref, shift_ref, frac_ref, face_ref, convect_ref, foot_ref, region_ref, out_ref, rows_ref, *scratch):
    f32, i32 = jnp.float32, jnp.int32
    sources = (sign_ref, foot_ref, region_ref, convect_ref, shift_ref, frac_ref, face_ref)
    held, arrived = scratch[:-1], scratch[-1]
    copies = [
        pltpu.make_async_copy(source, slot, arrived.at[n])
        for n, (source, slot) in enumerate(zip(sources, held))
    ]
    for copy in copies:
        copy.start()
    signs, foot, region, convect, shift, frac, face = held
    base = tracers * 2 * SUB
    for n, slot in ((1, foot), (2, region), (3, convect)):
        copies[n].wait()
        value = slot[...].astype(f32)
        out_ref[base + (n - 1) * SUB : base + n * SUB, :] = 0.5 * value if n == 3 else value
    for n in (4, 5, 6):
        copies[n].wait()
    ends = lax.axis_index("lat") == lax.axis_size("lat") - 1
    lane = lax.broadcasted_iota(i32, (2, LANES), 1)
    closed = jnp.where(ends, LANES - 1, LANES)
    a = frac[...]
    rows_ref[...] = jnp.concatenate(
        [
            shift[...].astype(f32),
            jnp.where(lane == closed, 0.0, face[...]),
            a * (a + 1.0) * 0.5,
            1.0 - a * a,
            a * (a - 1.0) * 0.5,
            jnp.zeros((6, LANES), f32),
        ],
        axis=0,
    )
    copies[0].wait()
    for t in range(tracers):
        for l in range(2):
            out_ref[(2 * t + l) * SUB : (2 * t + l + 1) * SUB, :] = (2 * signs[t, l] - 1).astype(f32)


def on_device(
    probe_signs,
    shift_cells,
    courant_frac,
    merid_coef,
    convect_frac,
    footprint,
    region_id,
    owner_slots,
    prior_slot,
):
    tracers, levels, width, rows = probe_signs.shape
    blocks, bands = lax.axis_size("lon"), lax.axis_size("lat")
    assert (levels, width, rows, bands) == (2, SUB, LANES, 2) and blocks & (blocks - 1) == 0
    regions = owner_slots.shape[0]
    f32 = jnp.float32
    anywhere = pl.BlockSpec(memory_space=pl.ANY)
    fields = (probe_signs, footprint, region_id, convect_frac, shift_cells, courant_frac, merid_coef)
    block, params = pl.pallas_call(
        functools.partial(pack_kernel, tracers),
        out_shape=(pltpu.VMEM((tracers * levels * width + 3 * SUB, rows), f32), pltpu.VMEM((2 * SUB, rows), f32)),
        in_specs=[anywhere] * 7,
        out_specs=[pl.BlockSpec(memory_space=pltpu.VMEM)] * 2,
        scratch_shapes=[pltpu.VMEM(x.shape, x.dtype) for x in fields] + [pltpu.SemaphoreType.DMA((7,))],
    )(probe_signs, shift_cells, courant_frac, merid_coef, convect_frac, footprint, region_id)
    own = jnp.concatenate([block] + [turned(block, k) for k in range(1, blocks)] + [params])
    other = swapped(own, "lat", 1)
    return pl.pallas_call(
        functools.partial(transport_kernel, tracers, blocks, regions),
        out_shape=jax.ShapeDtypeStruct(probe_signs.shape, f32),
        in_specs=[pl.BlockSpec(memory_space=pltpu.VMEM)] * 4,
        out_specs=pl.BlockSpec(memory_space=pltpu.VMEM),
        scratch_shapes=[pltpu.VMEM((blocks, tracers * SUB, 2 * LANES), f32)],
        compiler_params=pltpu.CompilerParams(vmem_limit_bytes=48 * 1024 * 1024),
    )(own, other, owner_slots.reshape(1, regions), prior_slot)


def solution(mesh):
    placed = (
        P(("probe", "trc"), None, "lon", "lat"),
        P(None, "lat"),
        P(None, "lat"),
        P(None, "lat"),
        P("lon", "lat"),
        P("lon", "lat"),
        P("lon", "lat"),
        P(),
        P("trc", None),
    )
    return jax.shard_map(
        on_device,
        mesh=mesh,
        in_specs=placed,
        out_specs=P(("probe", "trc"), None, "lon", "lat"),
        check_vma=False,
    )
```

```python
import functools

import jax
import jax.numpy as jnp
from jax import lax
from jax.experimental import pallas as pl
from jax.experimental.pallas import tpu as pltpu
from jax.sharding import PartitionSpec as P

SUB, LANES = 8, 128


def swapped(block, axis, k):
    size = lax.axis_size(axis)
    return lax.ppermute(block, axis, [(i, i ^ k) for i in range(size)])


def ring(i):
    return i ^ (i >> 1)


def turned(block, k):
    size = lax.axis_size("lon")
    spot = {ring(i): i for i in range(size)}
    return lax.ppermute(block, "lon", [(i, spot[(ring(i) + k) % size]) for i in range(size)])


def transport_kernel(tracers, blocks, regions, own_ref, other_ref, owner_ref, prior_ref, out_ref, flat_ref):
    f32, i32 = jnp.float32, jnp.int32
    me = lax.axis_index("lon")
    place = [(ring(me) - ring((me + b) % blocks)) % blocks if b else 0 for b in range(blocks)]
    bands = (own_ref, other_ref)
    cycle = blocks * SUB
    row = lax.broadcasted_iota(i32, (SUB, LANES), 0)
    lane = lax.broadcasted_iota(i32, (SUB, LANES), 1)
    first_row, last_row = row == 0, row == SUB - 1
    first_lane, last_lane = lane == 0, lane == LANES - 1
    base = tracers * 2 * SUB
    stride = base + 3 * SUB

    def tile(h, b, at):
        return bands[h][pl.ds(pl.multiple_of(place[b] * stride, SUB) + at, SUB), :]

    def full(h, at):
        return jnp.broadcast_to(bands[h][at : at + 1, :], (SUB, LANES))

    foot = [[tile(h, b, base) for h in range(2)] for b in range(blocks)]
    region = [[tile(h, b, base + SUB).astype(i32) for h in range(2)] for b in range(blocks)]
    half = [[tile(h, b, base + 2 * SUB) for h in range(2)] for b in range(blocks)]
    at = blocks * stride
    shift = [[full(h, at + l).astype(i32) for h in range(2)] for l in range(2)]
    face, w_left, w_centre, w_right = (
        [[full(h, at + 2 * n + l) for h in range(2)] for l in range(2)] for n in range(1, 5)
    )

    def north(v):
        r = [pltpu.roll(x, LANES - 1, 1) for x in v]
        return [jnp.where(last_lane, r[1], r[0]), jnp.where(last_lane, r[0], r[1])]

    def south(v):
        r = [pltpu.roll(x, 1, 1) for x in v]
        return [jnp.where(first_lane, r[1], r[0]), jnp.where(first_lane, r[0], r[1])]

    face_prev = [south(x) for x in face]
    face_mid = [[1.0 - face[l][h] - face_prev[l][h] for h in range(2)] for l in range(2)]

    def meridional(v, l, only=(0, 1)):
        n, s = north(v), south(v)
        return [face_mid[l][h] * v[h] + face[l][h] * n[h] + face_prev[l][h] * s[h] for h in only]

    steps = range((blocks - 1).bit_length())

    def bits(e):
        return [e & (1 << k) != 0 for k in steps]

    def plan(amount, ahead):
        whole, within = amount >> 3, amount & 7
        if ahead:
            crossed = (row < within).astype(i32)
            index = (row + within) & 7
        else:
            crossed = (row + within >= SUB).astype(i32)
            index = (row - within) & 7
        return bits(whole + crossed), index

    def pick(v, plan, sign, wanted):
        masks, index = plan
        need = list(wanted)
        chain = []
        for k in reversed(steps):
            chain.append(need)
            need = sorted({(b + d) % blocks for b in need for d in (0, sign << k)})
        current = {b: v[b] for b in need}
        for k, need in zip(steps, reversed(chain)):
            current = {b: jnp.where(masks[k], current[(b + (sign << k)) % blocks], current[b]) for b in need}
        return [jnp.take_along_axis(current[b], index, axis=0, mode="promise_in_bounds") for b in wanted]

    def beside(v):
        after = [pltpu.roll(jnp.where(first_row, v[(b + 1) % blocks], v[b]), SUB - 1, 0) for b in range(blocks)]
        before = [pltpu.roll(jnp.where(last_row, v[(b - 1) % blocks], v[b]), 1, 0) for b in range(blocks)]
        return before, after

    every = range(blocks)
    plan_adjoint = [[plan(shift[l][h], True) for h in range(2)] for l in range(2)]
    plan_first = [plan(shift[0][h], False) for h in range(2)]
    plan_second = [
        [[plan(shift[l][h] + d, False) for d in (1, 0, -1)] for h in range(2)] for l in range(2)
    ]

    def zonal_adjoint(v, l):
        result = []
        for h in range(2):
            q = pick([v[b][h] for b in every], plan_adjoint[l][h], 1, every)
            before, after = beside(q)
            result.append(
                [w_left[l][h] * after[b] + w_centre[l][h] * q[b] + w_right[l][h] * before[b] for b in every]
            )
        return [[result[h][b] for h in range(2)] for b in every]

    for t in range(tracers):
        v = [[[tile(h, b, (2 * t + l) * SUB) for h in range(2)] for b in every] for l in range(2)]
        mixed = [[], []]
        for b in every:
            d = [half[b][h] * (v[1][b][h] - v[0][b][h]) for h in range(2)]
            mixed[0].append(meridional([v[0][b][h] + d[h] for h in range(2)], 0))
            mixed[1].append(meridional([v[1][b][h] - d[h] for h in range(2)], 1))
        v = [zonal_adjoint(mixed[l], l) for l in range(2)]
        mixed = [
            meridional([v[0][b][h] + half[b][h] * (v[1][b][h] - v[0][b][h]) for h in range(2)], 0) for b in every
        ]
        v = zonal_adjoint(mixed, 0)
        for b in every:
            for h in range(2):
                flat_ref[b, t * SUB : (t + 1) * SUB, h * LANES : (h + 1) * LANES] = foot[b][h] * v[b][h]

    bf16 = jnp.bfloat16
    lines = tracers * SUB
    total = jnp.zeros((2 * lines, SUB * regions), f32)
    number = lax.broadcasted_iota(i32, (regions, 2 * LANES), 0).astype(bf16)[None]
    for b in every:
        x = flat_ref[b]
        hi = x.astype(bf16)
        rest = x - hi.astype(f32)
        mid = rest.astype(bf16)
        ids = jnp.concatenate(region[b], axis=1).astype(f32)
        ids = jnp.broadcast_to(ids[:, None, :], (SUB, regions, 2 * LANES)).astype(bf16)
        one, zero = jnp.ones((), bf16), jnp.zeros((), bf16)
        table = jnp.where(ids == number, one, zero).reshape(SUB * regions, 2 * LANES)
        total = total + lax.dot_general(
            jnp.concatenate([hi, mid], axis=0),
            table,
            (((1,), (1,)), ((), ())),
            preferred_element_type=f32,
        )
    sums = total[:lines] + total[lines : 2 * lines]
    width = SUB * regions
    column = lax.broadcasted_iota(i32, (SUB, width), 1)
    keep = column // regions == lax.broadcasted_iota(i32, (SUB, width), 0)
    sums = jnp.concatenate(
        [
            jnp.sum(jnp.where(keep, sums[t * SUB : (t + 1) * SUB], 0.0), axis=0, keepdims=True)
            for t in range(tracers)
        ],
        axis=0,
    )
    while width > max(regions, LANES):
        width //= 2
        sums = sums[:, :width] + sums[:, width:]
    period = width
    while period > regions:
        period //= 2
        sums = sums + pltpu.roll(sums, period, 1)
    spot = lax.broadcasted_iota(i32, (width, regions), 0) % regions
    holds = jnp.where(spot == owner_ref[...], 1.0, 0.0)
    prior = lax.dot_general(
        prior_ref[...],
        holds,
        (((1,), (1,)), ((), ())),
        precision=lax.Precision.HIGHEST,
        preferred_element_type=f32,
    )
    scaled = sums * prior

    keep0 = [[1.0 - x for x in y] for y in half]
    for t in range(tracers):
        rows = jnp.broadcast_to(scaled[t : t + 1], (SUB, width))

        def spread(ids):
            result = None
            for k in range(width // LANES):
                part = jnp.take_along_axis(
                    rows[:, k * LANES : (k + 1) * LANES], ids & (LANES - 1), axis=1, mode="promise_in_bounds"
                )
                result = part if k == 0 else jnp.where(ids >> 7 == k, part, result)
            return result

        v = [[foot[b][h] * spread(region[b][h]) for h in range(2)] for b in every]
        u = []
        for h in range(2):
            p = pick([v[b][h] for b in every], plan_first[h], -1, every)
            before, after = beside(p)
            u.append(
                [w_left[0][h] * before[b] + w_centre[0][h] * p[b] + w_right[0][h] * after[b] for b in every]
            )
        u = [meridional([u[h][b] for h in range(2)], 0) for b in every]
        pair = [
            [[keep0[b][h] * u[b][h] for h in range(2)] for b in every],
            [[half[b][h] * u[b][h] for h in range(2)] for b in every],
        ]
        moved = []
        for l in range(2):
            z = []
            for h in range(2):
                source = [pair[l][b][h] for b in every]
                before, centre, after = (pick(source, p, -1, [0])[0] for p in plan_second[l][h])
                z.append(w_left[l][h] * before + w_centre[l][h] * centre + w_right[l][h] * after)
            moved.append(meridional(z, l, (0,))[0])
        d = half[0][0] * (moved[1] - moved[0])
        out_ref[t, 0] = tile(0, 0, 2 * t * SUB) * (moved[0] + d)
        out_ref[t, 1] = tile(0, 0, (2 * t + 1) * SUB) * (moved[1] - d)


def pack_kernel(tracers, sign_ref, shift_ref, frac_ref, face_ref, convect_ref, foot_ref, region_ref, out_ref, rows_ref, *scratch):
    f32, i32 = jnp.float32, jnp.int32
    sources = (sign_ref, foot_ref, region_ref, convect_ref, shift_ref, frac_ref, face_ref)
    held, arrived = scratch[:-1], scratch[-1]
    copies = [
        pltpu.make_async_copy(source, slot, arrived.at[n])
        for n, (source, slot) in enumerate(zip(sources, held))
    ]
    for copy in copies:
        copy.start()
    signs, foot, region, convect, shift, frac, face = held
    base = tracers * 2 * SUB
    for n, slot in ((1, foot), (2, region), (3, convect)):
        copies[n].wait()
        value = slot[...].astype(f32)
        out_ref[base + (n - 1) * SUB : base + n * SUB, :] = 0.5 * value if n == 3 else value
    for n in (4, 5, 6):
        copies[n].wait()
    ends = lax.axis_index("lat") == lax.axis_size("lat") - 1
    lane = lax.broadcasted_iota(i32, (2, LANES), 1)
    closed = jnp.where(ends, LANES - 1, LANES)
    a = frac[...]
    rows_ref[...] = jnp.concatenate(
        [
            shift[...].astype(f32),
            jnp.where(lane == closed, 0.0, face[...]),
            a * (a + 1.0) * 0.5,
            1.0 - a * a,
            a * (a - 1.0) * 0.5,
            jnp.zeros((6, LANES), f32),
        ],
        axis=0,
    )
    copies[0].wait()
    for t in range(tracers):
        for l in range(2):
            out_ref[(2 * t + l) * SUB : (2 * t + l + 1) * SUB, :] = (2 * signs[t, l] - 1).astype(f32)


def on_device(
    probe_signs,
    shift_cells,
    courant_frac,
    merid_coef,
    convect_frac,
    footprint,
    region_id,
    owner_slots,
    prior_slot,
):
    tracers, levels, width, rows = probe_signs.shape
    blocks, bands = lax.axis_size("lon"), lax.axis_size("lat")
    assert (levels, width, rows, bands) == (2, SUB, LANES, 2) and blocks & (blocks - 1) == 0
    regions = owner_slots.shape[0]
    f32 = jnp.float32
    anywhere = pl.BlockSpec(memory_space=pl.ANY)
    fields = (probe_signs, footprint, region_id, convect_frac, shift_cells, courant_frac, merid_coef)
    block, params = pl.pallas_call(
        functools.partial(pack_kernel, tracers),
        out_shape=(pltpu.VMEM((tracers * levels * width + 3 * SUB, rows), f32), pltpu.VMEM((2 * SUB, rows), f32)),
        in_specs=[anywhere] * 7,
        out_specs=[pl.BlockSpec(memory_space=pltpu.VMEM)] * 2,
        scratch_shapes=[pltpu.VMEM(x.shape, x.dtype) for x in fields] + [pltpu.SemaphoreType.DMA((7,))],
    )(probe_signs, shift_cells, courant_frac, merid_coef, convect_frac, footprint, region_id)
    own = jnp.concatenate([block] + [turned(block, k) for k in range(1, blocks)] + [params])
    other = swapped(own, "lat", 1)
    return pl.pallas_call(
        functools.partial(transport_kernel, tracers, blocks, regions),
        out_shape=jax.ShapeDtypeStruct(probe_signs.shape, f32),
        in_specs=[pl.BlockSpec(memory_space=pltpu.VMEM)] * 4,
        out_specs=pl.BlockSpec(memory_space=pltpu.VMEM),
        scratch_shapes=[pltpu.VMEM((blocks, tracers * SUB, 2 * LANES), f32)],
        compiler_params=pltpu.CompilerParams(vmem_limit_bytes=48 * 1024 * 1024),
    )(own, other, owner_slots.reshape(1, regions), prior_slot)


def solution(mesh):
    placed = (
        P(("probe", "trc"), None, "lon", "lat"),
        P(None, "lat"),
        P(None, "lat"),
        P(None, "lat"),
        P("lon", "lat"),
        P("lon", "lat"),
        P("lon", "lat"),
        P(),
        P("trc", None),
    )
    return jax.shard_map(
        on_device,
        mesh=mesh,
        in_specs=placed,
        out_specs=P(("probe", "trc"), None, "lon", "lat"),
        check_vma=False,
    )
```

```python
import functools

import jax
import jax.numpy as jnp
from jax import lax
from jax.experimental import pallas as pl
from jax.experimental.pallas import tpu as pltpu
from jax.sharding import PartitionSpec as P

SUB, LANES = 8, 128


def swapped(block, axis, k):
    size = lax.axis_size(axis)
    return lax.ppermute(block, axis, [(i, i ^ k) for i in range(size)])


def ring(i):
    return i ^ (i >> 1)


def turned(block, k):
    size = lax.axis_size("lon")
    spot = {ring(i): i for i in range(size)}
    return lax.ppermute(block, "lon", [(i, spot[(ring(i) + k) % size]) for i in range(size)])


def transport_kernel(tracers, blocks, regions, own_ref, other_ref, owner_ref, prior_ref, out_ref, flat_ref, scaled_ref):
    f32, i32 = jnp.float32, jnp.int32
    me = lax.axis_index("lon")
    place = [(ring(me) - ring((me + b) % blocks)) % blocks if b else 0 for b in range(blocks)]
    bands = (own_ref, other_ref)
    cycle = blocks * SUB
    row = lax.broadcasted_iota(i32, (SUB, LANES), 0)
    lane = lax.broadcasted_iota(i32, (SUB, LANES), 1)
    first_row, last_row = row == 0, row == SUB - 1
    first_lane, last_lane = lane == 0, lane == LANES - 1
    base = tracers * 2 * SUB
    stride = base + 3 * SUB

    def tile(h, b, at):
        return bands[h][pl.ds(pl.multiple_of(place[b] * stride, SUB) + at, SUB), :]

    def full(h, at):
        return jnp.broadcast_to(bands[h][at : at + 1, :], (SUB, LANES))

    foot = [[tile(h, b, base) for h in range(2)] for b in range(blocks)]
    region = [[tile(h, b, base + SUB).astype(i32) for h in range(2)] for b in range(blocks)]
    half = [[tile(h, b, base + 2 * SUB) for h in range(2)] for b in range(blocks)]
    at = blocks * stride
    shift = [[full(h, at + l).astype(i32) for h in range(2)] for l in range(2)]
    face, w_left, w_centre, w_right = (
        [[full(h, at + 2 * n + l) for h in range(2)] for l in range(2)] for n in range(1, 5)
    )

    def north(v):
        r = [pltpu.roll(x, LANES - 1, 1) for x in v]
        return [jnp.where(last_lane, r[1], r[0]), jnp.where(last_lane, r[0], r[1])]

    def south(v):
        r = [pltpu.roll(x, 1, 1) for x in v]
        return [jnp.where(first_lane, r[1], r[0]), jnp.where(first_lane, r[0], r[1])]

    face_prev = [south(x) for x in face]
    face_mid = [[1.0 - face[l][h] - face_prev[l][h] for h in range(2)] for l in range(2)]

    def meridional(v, l, only=(0, 1)):
        n, s = north(v), south(v)
        return [face_mid[l][h] * v[h] + face[l][h] * n[h] + face_prev[l][h] * s[h] for h in only]

    steps = range((blocks - 1).bit_length())

    def bits(e):
        return [e & (1 << k) != 0 for k in steps]

    def plan(amount, ahead):
        whole, within = amount >> 3, amount & 7
        if ahead:
            crossed = (row < within).astype(i32)
            index = (row + within) & 7
        else:
            crossed = (row + within >= SUB).astype(i32)
            index = (row - within) & 7
        return bits(whole + crossed), index

    def pick(v, plan, sign, wanted):
        masks, index = plan
        need = list(wanted)
        chain = []
        for k in reversed(steps):
            chain.append(need)
            need = sorted({(b + d) % blocks for b in need for d in (0, sign << k)})
        current = {b: v[b] for b in need}
        for k, need in zip(steps, reversed(chain)):
            current = {b: jnp.where(masks[k], current[(b + (sign << k)) % blocks], current[b]) for b in need}
        return [jnp.take_along_axis(current[b], index, axis=0, mode="promise_in_bounds") for b in wanted]

    def beside(v):
        after = [pltpu.roll(jnp.where(first_row, v[(b + 1) % blocks], v[b]), SUB - 1, 0) for b in range(blocks)]
        before = [pltpu.roll(jnp.where(last_row, v[(b - 1) % blocks], v[b]), 1, 0) for b in range(blocks)]
        return before, after

    every = range(blocks)
    plan_adjoint = [[plan(shift[l][h], True) for h in range(2)] for l in range(2)]
    plan_first = [plan(shift[0][h], False) for h in range(2)]
    plan_second = [
        [[plan(shift[l][h] + d, False) for d in (1, 0, -1)] for h in range(2)] for l in range(2)
    ]

    def zonal_adjoint(v, l):
        result = []
        for h in range(2):
            q = pick([v[b][h] for b in every], plan_adjoint[l][h], 1, every)
            before, after = beside(q)
            result.append(
                [w_left[l][h] * after[b] + w_centre[l][h] * q[b] + w_right[l][h] * before[b] for b in every]
            )
        return [[result[h][b] for h in range(2)] for b in every]

    flat_ref[:, :, tracers * SUB :, :] = jnp.zeros((blocks, 2, (SUB - tracers) * SUB, LANES), f32)
    for t in range(tracers):
        v = [[[tile(h, b, (2 * t + l) * SUB) for h in range(2)] for b in every] for l in range(2)]
        mixed = [[], []]
        for b in every:
            d = [half[b][h] * (v[1][b][h] - v[0][b][h]) for h in range(2)]
            mixed[0].append(meridional([v[0][b][h] + d[h] for h in range(2)], 0))
            mixed[1].append(meridional([v[1][b][h] - d[h] for h in range(2)], 1))
        v = [zonal_adjoint(mixed[l], l) for l in range(2)]
        mixed = [
            meridional([v[0][b][h] + half[b][h] * (v[1][b][h] - v[0][b][h]) for h in range(2)], 0) for b in every
        ]
        v = zonal_adjoint(mixed, 0)
        for b in every:
            for h in range(2):
                flat_ref[b, h, t * SUB : (t + 1) * SUB, :] = foot[b][h] * v[b][h]

    bf16 = jnp.bfloat16
    number = lax.broadcasted_iota(i32, (regions, 2 * LANES), 0).astype(bf16)[None]
    one, zero = jnp.ones((), bf16), jnp.zeros((), bf16)
    total = jnp.zeros((2 * SUB, regions), f32)
    for b in every:
        ids = jnp.concatenate(region[b], axis=1).astype(f32)
        ids = jnp.broadcast_to(ids[:, None, :], (SUB, regions, 2 * LANES)).astype(bf16)
        table = jnp.where(ids == number, one, zero)
        parts = []
        for i in range(SUB):
            x = jnp.concatenate([flat_ref[b, h, pl.ds(i, SUB, stride=SUB), :] for h in range(2)], axis=1)
            high = x.astype(bf16).astype(f32)
            parts.append(jnp.concatenate([high, x - high], axis=0).astype(bf16))
        total = total + lax.dot_general(
            jnp.concatenate(parts, axis=1),
            jnp.concatenate([table[i] for i in range(SUB)], axis=1),
            (((1,), (1,)), ((), ())),
            preferred_element_type=f32,
        )
    spot = lax.broadcasted_iota(i32, (regions, regions), 0)
    holds = jnp.where(spot == owner_ref[...], 1.0, 0.0)
    prior = lax.dot_general(
        prior_ref[...],
        holds,
        (((1,), (1,)), ((), ())),
        precision=lax.Precision.HIGHEST,
        preferred_element_type=f32,
    )
    scaled_ref[:tracers, :regions] = (total[:SUB] + total[SUB:])[:tracers] * prior
    width = scaled_ref.shape[1]

    keep0 = [[1.0 - x for x in y] for y in half]
    for t in range(tracers):
        rows = jnp.broadcast_to(scaled_ref[t : t + 1, :], (SUB, width))

        def spread(ids):
            result = None
            for k in range(width // LANES):
                part = jnp.take_along_axis(
                    rows[:, k * LANES : (k + 1) * LANES], ids & (LANES - 1), axis=1, mode="promise_in_bounds"
                )
                result = part if k == 0 else jnp.where(ids >> 7 == k, part, result)
            return result

        v = [[foot[b][h] * spread(region[b][h]) for h in range(2)] for b in every]
        u = []
        for h in range(2):
            p = pick([v[b][h] for b in every], plan_first[h], -1, every)
            before, after = beside(p)
            u.append(
                [w_left[0][h] * before[b] + w_centre[0][h] * p[b] + w_right[0][h] * after[b] for b in every]
            )
        u = [meridional([u[h][b] for h in range(2)], 0) for b in every]
        pair = [
            [[keep0[b][h] * u[b][h] for h in range(2)] for b in every],
            [[half[b][h] * u[b][h] for h in range(2)] for b in every],
        ]
        moved = []
        for l in range(2):
            z = []
            for h in range(2):
                source = [pair[l][b][h] for b in every]
                before, centre, after = (pick(source, p, -1, [0])[0] for p in plan_second[l][h])
                z.append(w_left[l][h] * before + w_centre[l][h] * centre + w_right[l][h] * after)
            moved.append(meridional(z, l, (0,))[0])
        d = half[0][0] * (moved[1] - moved[0])
        out_ref[t, 0] = tile(0, 0, 2 * t * SUB) * (moved[0] + d)
        out_ref[t, 1] = tile(0, 0, (2 * t + 1) * SUB) * (moved[1] - d)


def pack_kernel(tracers, sign_ref, shift_ref, frac_ref, face_ref, convect_ref, foot_ref, region_ref, out_ref, rows_ref, *scratch):
    f32, i32 = jnp.float32, jnp.int32
    sources = (sign_ref, foot_ref, region_ref, convect_ref, shift_ref, frac_ref, face_ref)
    held, arrived = scratch[:-1], scratch[-1]
    copies = [
        pltpu.make_async_copy(source, slot, arrived.at[n])
        for n, (source, slot) in enumerate(zip(sources, held))
    ]
    for copy in copies:
        copy.start()
    signs, foot, region, convect, shift, frac, face = held
    base = tracers * 2 * SUB
    for n, slot in ((1, foot), (2, region), (3, convect)):
        copies[n].wait()
        value = slot[...].astype(f32)
        out_ref[base + (n - 1) * SUB : base + n * SUB, :] = 0.5 * value if n == 3 else value
    for n in (4, 5, 6):
        copies[n].wait()
    ends = lax.axis_index("lat") == lax.axis_size("lat") - 1
    lane = lax.broadcasted_iota(i32, (2, LANES), 1)
    closed = jnp.where(ends, LANES - 1, LANES)
    a = frac[...]
    rows_ref[...] = jnp.concatenate(
        [
            shift[...].astype(f32),
            jnp.where(lane == closed, 0.0, face[...]),
            a * (a + 1.0) * 0.5,
            1.0 - a * a,
            a * (a - 1.0) * 0.5,
            jnp.zeros((6, LANES), f32),
        ],
        axis=0,
    )
    copies[0].wait()
    for t in range(tracers):
        for l in range(2):
            out_ref[(2 * t + l) * SUB : (2 * t + l + 1) * SUB, :] = (2 * signs[t, l] - 1).astype(f32)


def on_device(
    probe_signs,
    shift_cells,
    courant_frac,
    merid_coef,
    convect_frac,
    footprint,
    region_id,
    owner_slots,
    prior_slot,
):
    tracers, levels, width, rows = probe_signs.shape
    blocks, bands = lax.axis_size("lon"), lax.axis_size("lat")
    assert (levels, width, rows, bands) == (2, SUB, LANES, 2) and blocks & (blocks - 1) == 0
    regions = owner_slots.shape[0]
    f32 = jnp.float32
    anywhere = pl.BlockSpec(memory_space=pl.ANY)
    fields = (probe_signs, footprint, region_id, convect_frac, shift_cells, courant_frac, merid_coef)
    block, params = pl.pallas_call(
        functools.partial(pack_kernel, tracers),
        out_shape=(pltpu.VMEM((tracers * levels * width + 3 * SUB, rows), f32), pltpu.VMEM((2 * SUB, rows), f32)),
        in_specs=[anywhere] * 7,
        out_specs=[pl.BlockSpec(memory_space=pltpu.VMEM)] * 2,
        scratch_shapes=[pltpu.VMEM(x.shape, x.dtype) for x in fields] + [pltpu.SemaphoreType.DMA((7,))],
    )(probe_signs, shift_cells, courant_frac, merid_coef, convect_frac, footprint, region_id)
    own = jnp.concatenate([block] + [turned(block, k) for k in range(1, blocks)] + [params])
    other = swapped(own, "lat", 1)
    return pl.pallas_call(
        functools.partial(transport_kernel, tracers, blocks, regions),
        out_shape=jax.ShapeDtypeStruct(probe_signs.shape, f32),
        in_specs=[pl.BlockSpec(memory_space=pltpu.VMEM)] * 4,
        out_specs=pl.BlockSpec(memory_space=pltpu.VMEM),
        scratch_shapes=[
            pltpu.VMEM((blocks, 2, SUB * SUB, LANES), f32),
            pltpu.VMEM((tracers, max(regions, LANES)), f32),
        ],
        compiler_params=pltpu.CompilerParams(vmem_limit_bytes=48 * 1024 * 1024),
    )(own, other, owner_slots.reshape(1, regions), prior_slot)


def solution(mesh):
    placed = (
        P(("probe", "trc"), None, "lon", "lat"),
        P(None, "lat"),
        P(None, "lat"),
        P(None, "lat"),
        P("lon", "lat"),
        P("lon", "lat"),
        P("lon", "lat"),
        P(),
        P("trc", None),
    )
    return jax.shard_map(
        on_device,
        mesh=mesh,
        in_specs=placed,
        out_specs=P(("probe", "trc"), None, "lon", "lat"),
        check_vma=False,
    )
```

```python
import functools

import jax
import jax.numpy as jnp
from jax import lax
from jax.experimental import pallas as pl
from jax.experimental.pallas import tpu as pltpu
from jax.sharding import PartitionSpec as P

SUB, LANES = 8, 128


def swapped(block, axis, k):
    size = lax.axis_size(axis)
    return lax.ppermute(block, axis, [(i, i ^ k) for i in range(size)])


def ring(i):
    return i ^ (i >> 1)


def turned(block, k):
    size = lax.axis_size("lon")
    spot = {ring(i): i for i in range(size)}
    return lax.ppermute(block, "lon", [(i, spot[(ring(i) + k) % size]) for i in range(size)])


def transport_kernel(tracers, blocks, regions, own_ref, other_ref, owner_ref, prior_ref, out_ref, flat_ref, scaled_ref):
    f32, i32 = jnp.float32, jnp.int32
    me = lax.axis_index("lon")
    place = [(ring(me) - ring((me + b) % blocks)) % blocks if b else 0 for b in range(blocks)]
    bands = (own_ref, other_ref)
    cycle = blocks * SUB
    row = lax.broadcasted_iota(i32, (SUB, LANES), 0)
    lane = lax.broadcasted_iota(i32, (SUB, LANES), 1)
    first_row, last_row = row == 0, row == SUB - 1
    first_lane, last_lane = lane == 0, lane == LANES - 1
    base = tracers * 2 * SUB
    stride = base + 3 * SUB

    def tile(h, b, at):
        return bands[h][pl.ds(pl.multiple_of(place[b] * stride, SUB) + at, SUB), :]

    def full(h, at):
        return jnp.broadcast_to(bands[h][at : at + 1, :], (SUB, LANES))

    foot = [[tile(h, b, base) for h in range(2)] for b in range(blocks)]
    region = [[tile(h, b, base + SUB).astype(i32) for h in range(2)] for b in range(blocks)]
    half = [[tile(h, b, base + 2 * SUB) for h in range(2)] for b in range(blocks)]
    at = blocks * stride
    shift = [[full(h, at + l).astype(i32) for h in range(2)] for l in range(2)]
    face, w_left, w_centre, w_right = (
        [[full(h, at + 2 * n + l) for h in range(2)] for l in range(2)] for n in range(1, 5)
    )

    def north(v):
        return [pltpu.roll(jnp.where(first_lane, v[1 - h], v[h]), LANES - 1, 1) for h in range(2)]

    def south(v):
        return [pltpu.roll(jnp.where(last_lane, v[1 - h], v[h]), 1, 1) for h in range(2)]

    face_prev = [south(x) for x in face]
    face_mid = [[1.0 - face[l][h] - face_prev[l][h] for h in range(2)] for l in range(2)]

    def meridional(v, l, only=(0, 1)):
        n, s = north(v), south(v)
        return [face_mid[l][h] * v[h] + face[l][h] * n[h] + face_prev[l][h] * s[h] for h in only]

    steps = range((blocks - 1).bit_length())

    def bits(e):
        return [e & (1 << k) != 0 for k in steps]

    def plan(amount, ahead):
        whole, within = amount >> 3, amount & 7
        if ahead:
            crossed = (row < within).astype(i32)
            index = (row + within) & 7
        else:
            crossed = (row + within >= SUB).astype(i32)
            index = (row - within) & 7
        return bits(whole + crossed), index

    def pick(v, plan, sign, wanted):
        masks, index = plan
        need = list(wanted)
        chain = []
        for k in reversed(steps):
            chain.append(need)
            need = sorted({(b + d) % blocks for b in need for d in (0, sign << k)})
        current = {b: v[b] for b in need}
        for k, need in zip(steps, reversed(chain)):
            current = {b: jnp.where(masks[k], current[(b + (sign << k)) % blocks], current[b]) for b in need}
        return [jnp.take_along_axis(current[b], index, axis=0, mode="promise_in_bounds") for b in wanted]

    def beside(v):
        after = [pltpu.roll(jnp.where(first_row, v[(b + 1) % blocks], v[b]), SUB - 1, 0) for b in range(blocks)]
        before = [pltpu.roll(jnp.where(last_row, v[(b - 1) % blocks], v[b]), 1, 0) for b in range(blocks)]
        return before, after

    every = range(blocks)
    plan_adjoint = [[plan(shift[l][h], True) for h in range(2)] for l in range(2)]
    plan_first = [plan(shift[0][h], False) for h in range(2)]
    plan_second = [
        [[plan(shift[l][h] + d, False) for d in (1, 0, -1)] for h in range(2)] for l in range(2)
    ]

    def zonal_adjoint(v, l):
        result = []
        for h in range(2):
            q = pick([v[b][h] for b in every], plan_adjoint[l][h], 1, every)
            before, after = beside(q)
            result.append(
                [w_left[l][h] * after[b] + w_centre[l][h] * q[b] + w_right[l][h] * before[b] for b in every]
            )
        return [[result[h][b] for h in range(2)] for b in every]

    flat_ref[:, :, tracers * SUB :, :] = jnp.zeros((blocks, 2, (SUB - tracers) * SUB, LANES), f32)
    for t in range(tracers):
        v = [[[tile(h, b, (2 * t + l) * SUB) for h in range(2)] for b in every] for l in range(2)]
        mixed = [[], []]
        for b in every:
            d = [half[b][h] * (v[1][b][h] - v[0][b][h]) for h in range(2)]
            mixed[0].append(meridional([v[0][b][h] + d[h] for h in range(2)], 0))
            mixed[1].append(meridional([v[1][b][h] - d[h] for h in range(2)], 1))
        v = [zonal_adjoint(mixed[l], l) for l in range(2)]
        mixed = [
            meridional([v[0][b][h] + half[b][h] * (v[1][b][h] - v[0][b][h]) for h in range(2)], 0) for b in every
        ]
        v = zonal_adjoint(mixed, 0)
        for b in every:
            for h in range(2):
                flat_ref[b, h, t * SUB : (t + 1) * SUB, :] = foot[b][h] * v[b][h]

    bf16 = jnp.bfloat16
    number = lax.broadcasted_iota(i32, (regions, 2 * LANES), 0).astype(bf16)[None]
    one, zero = jnp.ones((), bf16), jnp.zeros((), bf16)
    total = jnp.zeros((2 * SUB, regions), f32)
    for b in every:
        ids = jnp.concatenate(region[b], axis=1).astype(f32)
        ids = jnp.broadcast_to(ids[:, None, :], (SUB, regions, 2 * LANES)).astype(bf16)
        table = jnp.where(ids == number, one, zero)
        parts = []
        for i in range(SUB):
            x = jnp.concatenate([flat_ref[b, h, pl.ds(i, SUB, stride=SUB), :] for h in range(2)], axis=1)
            high = x.astype(bf16).astype(f32)
            parts.append(jnp.concatenate([high, x - high], axis=0).astype(bf16))
        total = total + lax.dot_general(
            jnp.concatenate(parts, axis=1),
            jnp.concatenate([table[i] for i in range(SUB)], axis=1),
            (((1,), (1,)), ((), ())),
            preferred_element_type=f32,
        )
    spot = lax.broadcasted_iota(i32, (regions, regions), 0)
    holds = jnp.where(spot == owner_ref[...], 1.0, 0.0)
    prior = lax.dot_general(
        prior_ref[...],
        holds,
        (((1,), (1,)), ((), ())),
        precision=lax.Precision.HIGHEST,
        preferred_element_type=f32,
    )
    scaled_ref[:tracers, :regions] = (total[:SUB] + total[SUB:])[:tracers] * prior
    width = scaled_ref.shape[1]

    keep0 = [[1.0 - x for x in y] for y in half]
    for t in range(tracers):
        rows = jnp.broadcast_to(scaled_ref[t : t + 1, :], (SUB, width))

        def spread(ids):
            result = None
            for k in range(width // LANES):
                part = jnp.take_along_axis(
                    rows[:, k * LANES : (k + 1) * LANES], ids & (LANES - 1), axis=1, mode="promise_in_bounds"
                )
                result = part if k == 0 else jnp.where(ids >> 7 == k, part, result)
            return result

        v = [[foot[b][h] * spread(region[b][h]) for h in range(2)] for b in every]
        u = []
        for h in range(2):
            p = pick([v[b][h] for b in every], plan_first[h], -1, every)
            before, after = beside(p)
            u.append(
                [w_left[0][h] * before[b] + w_centre[0][h] * p[b] + w_right[0][h] * after[b] for b in every]
            )
        u = [meridional([u[h][b] for h in range(2)], 0) for b in every]
        pair = [
            [[keep0[b][h] * u[b][h] for h in range(2)] for b in every],
            [[half[b][h] * u[b][h] for h in range(2)] for b in every],
        ]
        moved = []
        for l in range(2):
            z = []
            for h in range(2):
                source = [pair[l][b][h] for b in every]
                before, centre, after = (pick(source, p, -1, [0])[0] for p in plan_second[l][h])
                z.append(w_left[l][h] * before + w_centre[l][h] * centre + w_right[l][h] * after)
            moved.append(meridional(z, l, (0,))[0])
        d = half[0][0] * (moved[1] - moved[0])
        out_ref[t, 0] = tile(0, 0, 2 * t * SUB) * (moved[0] + d)
        out_ref[t, 1] = tile(0, 0, (2 * t + 1) * SUB) * (moved[1] - d)


def pack_kernel(tracers, sign_ref, shift_ref, frac_ref, face_ref, convect_ref, foot_ref, region_ref, out_ref, rows_ref, *scratch):
    f32, i32 = jnp.float32, jnp.int32
    sources = (sign_ref, foot_ref, region_ref, convect_ref, shift_ref, frac_ref, face_ref)
    held, arrived = scratch[:-1], scratch[-1]
    copies = [
        pltpu.make_async_copy(source, slot, arrived.at[n])
        for n, (source, slot) in enumerate(zip(sources, held))
    ]
    for copy in copies:
        copy.start()
    signs, foot, region, convect, shift, frac, face = held
    base = tracers * 2 * SUB
    for n, slot in ((1, foot), (2, region), (3, convect)):
        copies[n].wait()
        value = slot[...].astype(f32)
        out_ref[base + (n - 1) * SUB : base + n * SUB, :] = 0.5 * value if n == 3 else value
    for n in (4, 5, 6):
        copies[n].wait()
    ends = lax.axis_index("lat") == lax.axis_size("lat") - 1
    lane = lax.broadcasted_iota(i32, (2, LANES), 1)
    closed = jnp.where(ends, LANES - 1, LANES)
    a = frac[...]
    rows_ref[...] = jnp.concatenate(
        [
            shift[...].astype(f32),
            jnp.where(lane == closed, 0.0, face[...]),
            a * (a + 1.0) * 0.5,
            1.0 - a * a,
            a * (a - 1.0) * 0.5,
            jnp.zeros((6, LANES), f32),
        ],
        axis=0,
    )
    copies[0].wait()
    for t in range(tracers):
        for l in range(2):
            out_ref[(2 * t + l) * SUB : (2 * t + l + 1) * SUB, :] = (2 * signs[t, l] - 1).astype(f32)


def on_device(
    probe_signs,
    shift_cells,
    courant_frac,
    merid_coef,
    convect_frac,
    footprint,
    region_id,
    owner_slots,
    prior_slot,
):
    tracers, levels, width, rows = probe_signs.shape
    blocks, bands = lax.axis_size("lon"), lax.axis_size("lat")
    assert (levels, width, rows, bands) == (2, SUB, LANES, 2) and blocks & (blocks - 1) == 0
    regions = owner_slots.shape[0]
    f32 = jnp.float32
    anywhere = pl.BlockSpec(memory_space=pl.ANY)
    fields = (probe_signs, footprint, region_id, convect_frac, shift_cells, courant_frac, merid_coef)
    block, params = pl.pallas_call(
        functools.partial(pack_kernel, tracers),
        out_shape=(pltpu.VMEM((tracers * levels * width + 3 * SUB, rows), f32), pltpu.VMEM((2 * SUB, rows), f32)),
        in_specs=[anywhere] * 7,
        out_specs=[pl.BlockSpec(memory_space=pltpu.VMEM)] * 2,
        scratch_shapes=[pltpu.VMEM(x.shape, x.dtype) for x in fields] + [pltpu.SemaphoreType.DMA((7,))],
    )(probe_signs, shift_cells, courant_frac, merid_coef, convect_frac, footprint, region_id)
    own = jnp.concatenate([block] + [turned(block, k) for k in range(1, blocks)] + [params])
    other = swapped(own, "lat", 1)
    return pl.pallas_call(
        functools.partial(transport_kernel, tracers, blocks, regions),
        out_shape=jax.ShapeDtypeStruct(probe_signs.shape, f32),
        in_specs=[pl.BlockSpec(memory_space=pltpu.VMEM)] * 4,
        out_specs=pl.BlockSpec(memory_space=pltpu.VMEM),
        scratch_shapes=[
            pltpu.VMEM((blocks, 2, SUB * SUB, LANES), f32),
            pltpu.VMEM((tracers, max(regions, LANES)), f32),
        ],
        compiler_params=pltpu.CompilerParams(vmem_limit_bytes=48 * 1024 * 1024),
    )(own, other, owner_slots.reshape(1, regions), prior_slot)


def solution(mesh):
    placed = (
        P(("probe", "trc"), None, "lon", "lat"),
        P(None, "lat"),
        P(None, "lat"),
        P(None, "lat"),
        P("lon", "lat"),
        P("lon", "lat"),
        P("lon", "lat"),
        P(),
        P("trc", None),
    )
    return jax.shard_map(
        on_device,
        mesh=mesh,
        in_specs=placed,
        out_specs=P(("probe", "trc"), None, "lon", "lat"),
        check_vma=False,
    )
```
